32 devices in a mesh: wide: 16 (over z, y, x), narrow: 2 (over core).
Axes of the slice: x: 2, y: 2, z: 4, core: 2. Of those that a mesh axis runs over, the one named last changes fastest.
Arguments:
- sublevel_symbol_entries: bfloat16 [1024, 4, 4096], P('wide', None, 'narrow'), may hold values from -160 to 160
- prior_symbol_memory: bfloat16 [1024, 4096], P('wide', 'narrow'), may hold values from -6 to 6
- entry_scaling_multiplier: float32 [4096], P('narrow'), may hold values from 0.25 to 1.75
- entry_scaling_offset: float32 [4096], P('narrow'), may hold values from -4 to 4
- learned_blending: float32 [6, 4096], P(None, 'narrow'), may hold values from 0 to 1
- blending_lowering_coefficients: bfloat16 [4096, 160], P('narrow'), may hold values from -0.09375 to 0.09375
- blending_raising_coefficients: bfloat16 [5, 32, 4096], P(None, None, 'narrow'), may hold values from -1 to 1
- fading_lowering_coefficients: bfloat16 [4096, 64], P('narrow'), may hold values from -0.09375 to 0.09375
- fading_raising_coefficients: bfloat16 [64, 4096], P(None, 'wide'), may hold values from -0.75 to 0.75
- learned_fading: float32 [4096], P('wide'), may hold values from -6 to 1
- immediate_item_premium: float32 [4096], P('wide'), may hold values from -3 to 3
- acceptor_projection: bfloat16 [4096, 4096], P('narrow', 'wide'), may hold values from -0.09375 to 0.09375
- lookup_projection: bfloat16 [4096, 4096], P('narrow', 'wide'), may hold values from -0.09375 to 0.09375
- payload_projection: bfloat16 [4096, 4096], P('narrow', 'wide'), may hold values from -0.09375 to 0.09375
- gating_projection: bfloat16 [4096, 4096], P('narrow', 'wide'), may hold values from -0.09375 to 0.09375
- emission_projection: bfloat16 [4096, 4096], P(None, 'wide'), may hold values from -0.09375 to 0.09375
- group_scaling_multiplier: float32 [4096], P('wide'), may hold values from 0.25 to 1.75
- group_scaling_offset: float32 [4096], P('wide'), may hold values from -4 to 4
- dialogue_group_memory: float32 [262144, 1024], P('wide', 'narrow'), may hold values from -6 to 6
Outputs:
- mixing_output: bfloat16 [1024, 4, 4096], P('narrow', None, 'wide')
- final_state: float32 [262144, 1024], P('wide', 'narrow')
The draws below stay inside these ranges and needn't reach their ends.
All inputs are finite; a program needn't handle non-finite values.
Results may differ from the reference program's by a relative error of at most 0.034.
Values may be sent and summed in bfloat16 or wider, within the bound.
No kernel may reach another device: no remote copies, remote signals or barrier semaphores. Data moves between devices by JAX's collectives and lax.ppermute only.
A program may use at most 320 MiB of HBM per device.

```python
import math
import jax
import jax.numpy as jnp
from jax import lax

NUM_CHANNEL_SETS = 64
CHANNEL_SPAN = 64
MIXING_RANK = 32
DECAY_RANK = 64
PARALLEL_CHATS = 1024
DECODE_MOVES = 4
FEATURE_EXTENT = 4096
N_NARROW = 2


def feature_draw(key, shape):
    first, second, third = jax.random.split(key, 3)
    columns = shape[-1]
    ramp = 3.0 ** (jnp.arange(columns, dtype=jnp.float32) / columns)
    column_scale = ramp * jnp.exp(jax.random.uniform(first, (columns,), jnp.float32, 0.0, math.log(3.3)))
    row_scale = jnp.exp(jax.random.uniform(second, (shape[0],) + (1,) * (len(shape) - 1), jnp.float32, 0.0, math.log(10.0)))
    base = jnp.clip(jax.random.normal(third, shape, jnp.float32), -5.0, 5.0)
    return (base * column_scale * row_scale * 0.3).astype(jnp.bfloat16)


def draw_sublevel_symbol_entries(key, part):
    return feature_draw(jax.random.fold_in(key, 11), (PARALLEL_CHATS, DECODE_MOVES, FEATURE_EXTENT))


def block_levels(own_key, shape, pieces, low, top_value):
    level, own = 1.0, jax.random.fold_in(own_key, 6)
    for position, parts in pieces:
        steps = jnp.exp(jax.random.uniform(jax.random.fold_in(own, position), (parts,), jnp.float32, low / len(pieces), top_value / len(pieces)))
        level = level * jnp.repeat(steps, shape[position] // parts).reshape([-1 if axis == position else 1 for axis in range(len(shape))])
    return level


def bell_draw(key, dims, scale, most, cuts=(), held_as=jnp.bfloat16):
    gain = block_levels(key, dims, cuts, -0.22, 0.18) if cuts else 1.0
    values = jax.random.normal(key, dims, jnp.float32) * scale * gain
    return jnp.minimum(jnp.maximum(values, -most), most).astype(held_as)


def setup_inputs(seed: int = 0) -> dict:
    key_of = jax.random.split(jax.random.key(seed), 20)
    sublevel_symbol_entries = draw_sublevel_symbol_entries(jax.random.fold_in(key_of[19], 71), 0)
    prior_symbol_memory = bell_draw(key_of[1], (PARALLEL_CHATS, FEATURE_EXTENT), 1.0, 6.0, ((0, 16), (1, 2)))
    entry_scaling_multiplier = jnp.clip(1.0 + 0.15 * jax.random.normal(key_of[2], (FEATURE_EXTENT,), jnp.float32), 0.25, 1.75)
    entry_scaling_offset = bell_draw(key_of[3], (FEATURE_EXTENT,), 0.3, 4.0, ((0, 2),), jnp.float32)
    learned_blending = jnp.clip(1.0 * jax.random.uniform(key_of[4], (6, FEATURE_EXTENT), jnp.float32) ** block_levels(key_of[4], (6, FEATURE_EXTENT), ((1, 2),), -0.2, 0.2), 0.0, 1.0)
    blending_lowering_coefficients = bell_draw(key_of[5], (FEATURE_EXTENT, 5 * MIXING_RANK), FEATURE_EXTENT ** -0.5, 0.09375, ((0, 2),))
    blending_raising_coefficients = bell_draw(key_of[6], (5, MIXING_RANK, FEATURE_EXTENT), MIXING_RANK ** -0.5, 1.0, ((2, 2),))
    fading_lowering_coefficients = bell_draw(key_of[7], (FEATURE_EXTENT, DECAY_RANK), FEATURE_EXTENT ** -0.5, 0.09375, ((0, 2),))
    fading_raising_coefficients = bell_draw(key_of[8], (DECAY_RANK, FEATURE_EXTENT), DECAY_RANK ** -0.5, 0.75, ((1, 16),))
    learned_fading = jnp.clip(-6.0 + 7.0 * jax.random.uniform(key_of[9], (FEATURE_EXTENT,), jnp.float32) ** block_levels(key_of[9], (FEATURE_EXTENT,), ((0, 16),), -0.2, 0.2), -6.0, 1.0)
    immediate_item_premium = bell_draw(key_of[10], (FEATURE_EXTENT,), 0.5, 3.0, ((0, 16),), jnp.float32)
    acceptor_projection = bell_draw(key_of[11], (FEATURE_EXTENT, FEATURE_EXTENT), FEATURE_EXTENT ** -0.5, 0.09375, ((0, 2), (1, 16)))
    lookup_projection = bell_draw(key_of[12], (FEATURE_EXTENT, FEATURE_EXTENT), FEATURE_EXTENT ** -0.5, 0.09375, ((0, 2), (1, 16)))
    payload_projection = bell_draw(key_of[13], (FEATURE_EXTENT, FEATURE_EXTENT), FEATURE_EXTENT ** -0.5, 0.09375, ((0, 2), (1, 16)))
    gating_projection = bell_draw(key_of[14], (FEATURE_EXTENT, FEATURE_EXTENT), FEATURE_EXTENT ** -0.5, 0.09375, ((0, 2), (1, 16)))
    emission_projection = bell_draw(key_of[15], (FEATURE_EXTENT, FEATURE_EXTENT), FEATURE_EXTENT ** -0.5, 0.09375, ((1, 16),))
    group_scaling_multiplier = jnp.clip(1.0 + 0.15 * jax.random.normal(key_of[16], (FEATURE_EXTENT,), jnp.float32), 0.25, 1.75)
    group_scaling_offset = bell_draw(key_of[17], (FEATURE_EXTENT,), 0.3, 4.0, ((0, 16),), jnp.float32)
    dialogue_group_memory = bell_draw(key_of[18], (FEATURE_EXTENT * CHANNEL_SPAN, PARALLEL_CHATS), 1.0, 6.0, ((0, 16), (1, 2)), jnp.float32)
    return dict(sublevel_symbol_entries=sublevel_symbol_entries, prior_symbol_memory=prior_symbol_memory, entry_scaling_multiplier=entry_scaling_multiplier, entry_scaling_offset=entry_scaling_offset, learned_blending=learned_blending, blending_lowering_coefficients=blending_lowering_coefficients, blending_raising_coefficients=blending_raising_coefficients, fading_lowering_coefficients=fading_lowering_coefficients, fading_raising_coefficients=fading_raising_coefficients, learned_fading=learned_fading, immediate_item_premium=immediate_item_premium, acceptor_projection=acceptor_projection, lookup_projection=lookup_projection, payload_projection=payload_projection, gating_projection=gating_projection, emission_projection=emission_projection, group_scaling_multiplier=group_scaling_multiplier, group_scaling_offset=group_scaling_offset, dialogue_group_memory=dialogue_group_memory)


def flattened_product(left, right):
    shape = left.shape
    result = jnp.dot(left.reshape(-1, shape[-1]), right, preferred_element_type=jnp.float32)
    return result.reshape(shape[:-1] + (right.shape[-1],))

def blocked_dot(left, right):
    width = left.shape[-1] // N_NARROW
    total = jnp.zeros(left.shape[:-1] + (right.shape[-1],), jnp.float32)
    for block in range(N_NARROW):
        term = flattened_product(left[..., block * width:(block + 1) * width], right[block * width:(block + 1) * width])
        total = total + lax.optimization_barrier(term.astype(jnp.bfloat16)).astype(jnp.float32)
    return total

def solitary_channel_set(entry_lines):
    acceptor_lines, group_lookup, group_payload, retention_multiplier, present_symbol, group_reward = entry_lines
    outputs = []
    for index in range(DECODE_MOVES):
        present_acceptor = acceptor_lines[:, index].T
        key_now = group_lookup[:, index].T
        value_now = group_payload[:, index].T
        forget_now = retention_multiplier[:, index].T
        dyadic_tensor = key_now[:, None, :] * value_now[None, :, :]
        memory_retrieval = lax.optimization_barrier(jnp.sum(present_acceptor[:, None, :] * (present_symbol + group_reward[:, None, None] * dyadic_tensor), 0))
        present_symbol = forget_now[:, None, :] * present_symbol + dyadic_tensor
        center = lax.optimization_barrier(jnp.mean(memory_retrieval, 0, keepdims=True))
        offset = memory_retrieval - center
        outputs.append(offset * lax.rsqrt(lax.optimization_barrier(jnp.mean(offset * offset, 0, keepdims=True)) + 0.00064))
    return (jnp.stack(outputs, 0), present_symbol)

def reference(sublevel_symbol_entries, prior_symbol_memory, entry_scaling_multiplier, entry_scaling_offset, learned_blending, blending_lowering_coefficients, blending_raising_coefficients, fading_lowering_coefficients, fading_raising_coefficients, learned_fading, immediate_item_premium, acceptor_projection, lookup_projection, payload_projection, gating_projection, emission_projection, group_scaling_multiplier, group_scaling_offset, dialogue_group_memory):
    floats = sublevel_symbol_entries.astype(jnp.float32)
    center = lax.optimization_barrier(jnp.sum(floats, -1, keepdims=True)) / FEATURE_EXTENT
    spread = lax.optimization_barrier(jnp.sum(floats * floats, -1, keepdims=True)) / FEATURE_EXTENT - center * center
    normed = ((floats - center) * lax.rsqrt(spread + 1e-05) * entry_scaling_multiplier + entry_scaling_offset).astype(jnp.bfloat16)
    previous = jnp.concatenate([prior_symbol_memory[:, None], normed[:, :-1]], 1)
    normalized_float = normed.astype(jnp.float32)
    shifted_input = previous.astype(jnp.float32) - normalized_float
    blended = (normalized_float + shifted_input * learned_blending[0]).astype(jnp.bfloat16)
    hidden_activation = jnp.tanh(flattened_product(blended, blending_lowering_coefficients)).astype(jnp.bfloat16)
    mixing_values = []
    for selector_index in range(5):
        low_rank_update = flattened_product(hidden_activation[..., selector_index * MIXING_RANK:(selector_index + 1) * MIXING_RANK], blending_raising_coefficients[selector_index])
        mixing_values.append((normalized_float + shifted_input * (learned_blending[selector_index + 1] + low_rank_update)).astype(jnp.bfloat16))
    decay_hidden = jnp.tanh(flattened_product(mixing_values[0], fading_lowering_coefficients)).astype(jnp.bfloat16)
    shrink_coefficient = jnp.exp(-jnp.exp(learned_fading + flattened_product(decay_hidden, fading_raising_coefficients)))
    weights = (acceptor_projection, lookup_projection, payload_projection, gating_projection)
    transformed_outcome = [blocked_dot(mixing_values[selector_index + 1], weights[selector_index]) for selector_index in range(4)]

    def channel_set_first(array):
        return array.reshape(PARALLEL_CHATS, DECODE_MOVES, NUM_CHANNEL_SETS, CHANNEL_SPAN).transpose(2, 0, 1, 3)
    channel_set_recalls = dialogue_group_memory.reshape(NUM_CHANNEL_SETS, CHANNEL_SPAN, CHANNEL_SPAN, PARALLEL_CHATS)
    recalled_vectors, concluding_outcome = lax.map(solitary_channel_set, (channel_set_first(transformed_outcome[0]), channel_set_first(transformed_outcome[1]), channel_set_first(transformed_outcome[2]), channel_set_first(shrink_coefficient), channel_set_recalls, immediate_item_premium.reshape(NUM_CHANNEL_SETS, CHANNEL_SPAN)))
    squashed_vector = recalled_vectors.transpose(3, 1, 0, 2).reshape(PARALLEL_CHATS, DECODE_MOVES, FEATURE_EXTENT)
    gated = ((squashed_vector * group_scaling_multiplier + group_scaling_offset) * jax.nn.silu(transformed_outcome[3])).astype(jnp.bfloat16)
    mixing_output = flattened_product(gated, emission_projection).astype(jnp.bfloat16)
    return (mixing_output, concluding_outcome.reshape(FEATURE_EXTENT * CHANNEL_SPAN, PARALLEL_CHATS))
```

```python
import functools
import jax
import jax.numpy as jnp
from jax import lax
from jax.experimental import pallas as pl
from jax.experimental.pallas import tpu as pltpu
from jax.sharding import PartitionSpec as P

CHANNEL_SPAN = 64
FEATURE_EXTENT = 4096


def plain_device(
    sublevel_symbol_entries,
    prior_symbol_memory,
    entry_scaling_multiplier,
    entry_scaling_offset,
    learned_blending,
    blending_lowering_coefficients,
    blending_raising_coefficients,
    fading_lowering_coefficients,
    fading_raising_coefficients,
    learned_fading,
    immediate_item_premium,
    acceptor_projection,
    lookup_projection,
    payload_projection,
    gating_projection,
    emission_projection,
    group_scaling_multiplier,
    group_scaling_offset,
    dialogue_group_memory,
):
    rank = blending_raising_coefficients.shape[1]
    narrow_rows = dialogue_group_memory.shape[1]
    local_width = emission_projection.shape[1]
    group_partition = local_width // CHANNEL_SPAN
    weights = (acceptor_projection, lookup_projection, payload_projection, gating_projection)
    shift_gathered = lax.all_gather(prior_symbol_memory, "wide", axis=0, tiled=True)

    def channel_set_first(block):
        return block.reshape(narrow_rows, group_partition, CHANNEL_SPAN).transpose(1, 2, 0)

    present_symbol = dialogue_group_memory.reshape(
        group_partition, CHANNEL_SPAN, CHANNEL_SPAN, narrow_rows
    )
    previous_rows = prior_symbol_memory
    previous_all = shift_gathered
    results = []
    for index in range(sublevel_symbol_entries.shape[1]):
        floats = sublevel_symbol_entries[:, index : index + 1].astype(jnp.float32)
        totals, squares = lax.psum((jnp.sum(floats, -1), jnp.sum(floats * floats, -1)), "narrow")
        prepare_center = totals[..., None] / FEATURE_EXTENT
        spread = squares[..., None] / FEATURE_EXTENT - prepare_center * prepare_center
        normed = (
            (floats - prepare_center) * lax.rsqrt(spread + 1e-05) * entry_scaling_multiplier
            + entry_scaling_offset
        ).astype(jnp.bfloat16)
        previous = jnp.concatenate([previous_rows[:, None], normed[:, :-1]], 1)
        prepare_normalized_float = normed.astype(jnp.float32)
        prepare_shifted_input = previous.astype(jnp.float32) - prepare_normalized_float
        blended = (prepare_normalized_float + prepare_shifted_input * learned_blending[0]).astype(
            jnp.bfloat16
        )
        partial_mix = jnp.einsum(
            "smd,dr->smr",
            blended,
            blending_lowering_coefficients,
            preferred_element_type=jnp.float32,
        )
        hidden_activation = jnp.tanh(lax.psum(partial_mix, "narrow")).astype(jnp.bfloat16)
        decay_shift = jnp.einsum(
            "smr,rd->smd",
            hidden_activation[..., :rank],
            blending_raising_coefficients[0],
            preferred_element_type=jnp.float32,
        )
        decay_mix = (
            prepare_normalized_float + prepare_shifted_input * (learned_blending[1] + decay_shift)
        ).astype(jnp.bfloat16)
        partial_decay = jnp.einsum(
            "smd,dr->smr",
            decay_mix,
            fading_lowering_coefficients,
            preferred_element_type=jnp.float32,
        )
        decay_hidden = jnp.tanh(lax.psum(partial_decay, "narrow")).astype(jnp.bfloat16)
        small = jnp.concatenate([hidden_activation[..., rank:], decay_hidden], -1)
        prepare_normed_all = lax.all_gather(normed, "wide", axis=0, tiled=True)
        prepare_small_all = lax.all_gather(small, "wide", axis=0, tiled=True)
        normed, normed_all, small_all = (normed, prepare_normed_all, prepare_small_all)
        project_previous_all = previous_all[:, None]
        normalized_float = normed_all.astype(jnp.float32)
        shifted_input = project_previous_all.astype(jnp.float32) - normalized_float
        term_results = []
        for selector_index in range(4):
            low_rank_update = jnp.einsum(
                "smr,rd->smd",
                small_all[..., selector_index * rank : (selector_index + 1) * rank],
                blending_raising_coefficients[selector_index + 1],
                preferred_element_type=jnp.float32,
            )
            mixed_input = (
                normalized_float
                + shifted_input * (learned_blending[selector_index + 2] + low_rank_update)
            ).astype(jnp.bfloat16)
            term_results.append(
                jnp.einsum(
                    "smd,de->sme",
                    mixed_input,
                    weights[selector_index],
                    preferred_element_type=jnp.float32,
                )
            )
        project_transformed_outcome = lax.psum_scatter(
            jnp.concatenate(term_results, -1).astype(jnp.bfloat16),
            "narrow",
            scatter_dimension=0,
            tiled=True,
        ).astype(jnp.float32)
        rows_start = lax.axis_index("narrow") * narrow_rows
        decay_rows = lax.dynamic_slice_in_dim(
            small_all[..., 4 * rank :], rows_start, narrow_rows, 0
        )
        decay_log = learned_fading + jnp.einsum(
            "smr,rd->smd",
            decay_rows,
            fading_raising_coefficients,
            preferred_element_type=jnp.float32,
        )
        shrink_coefficient = jnp.exp(-jnp.exp(decay_log))
        recurrence_present_symbol = present_symbol
        each_group_reward = immediate_item_premium.reshape(group_partition, CHANNEL_SPAN)
        present_acceptor = channel_set_first(project_transformed_outcome[:, 0, :local_width])
        key_now = channel_set_first(
            project_transformed_outcome[:, 0, local_width : 2 * local_width]
        )
        value_now = channel_set_first(
            project_transformed_outcome[:, 0, 2 * local_width : 3 * local_width]
        )
        gate_now = project_transformed_outcome[:, 0, 3 * local_width :]
        forget_now = channel_set_first(shrink_coefficient[:, 0])
        dyadic_tensor = key_now[:, :, None, :] * value_now[:, None, :, :]
        memory_retrieval = jnp.sum(
            present_acceptor[:, :, None, :]
            * (recurrence_present_symbol + each_group_reward[:, :, None, None] * dyadic_tensor),
            1,
        )
        recurrence_present_symbol = (
            forget_now[:, :, None, :] * recurrence_present_symbol + dyadic_tensor
        )
        center = jnp.mean(memory_retrieval, 1, keepdims=True)
        offset = memory_retrieval - center
        scaled = offset * lax.rsqrt(jnp.mean(offset * offset, 1, keepdims=True) + 0.00064)
        squashed_vector = scaled.transpose(2, 0, 1).reshape(narrow_rows, local_width)
        pieces = [
            (
                (squashed_vector * group_scaling_multiplier + group_scaling_offset)
                * jax.nn.silu(gate_now)
            ).astype(jnp.bfloat16)
        ]
        present_symbol = recurrence_present_symbol
        gated = jnp.stack(pieces, 1)
        results.append(
            jnp.einsum(
                "smc,ce->sme",
                lax.all_gather(gated, "wide", axis=2, tiled=True),
                emission_projection,
                preferred_element_type=jnp.float32,
            ).astype(jnp.bfloat16)
        )
        previous_rows = normed[:, 0]
        previous_all = normed_all[:, 0]
    mixing_output = jnp.concatenate(results, 1)
    return (
        mixing_output,
        present_symbol.reshape(group_partition * CHANNEL_SPAN * CHANNEL_SPAN, narrow_rows),
    )


PLANES = 4
F32 = jnp.float32
BF16 = jnp.bfloat16


def pairs(move):
    moved = [(here, move(here)) for here in range(4 * PLANES)]
    return [(here, there) for here, there in moved if there is not None]


def x_mate(here):
    return here ^ 1


def y_mate(here):
    return here ^ 2


def z_mate(here):
    return here ^ 4


def z_middle(here):
    return {1: here + 4, 2: here - 4}.get(here // 4)


def z_outward(here):
    return {1: here - 4, 2: here + 4}.get(here // 4)


def z_shift(amount):
    return lambda here: (here + 4 * amount) % (4 * PLANES)


def send(block, move):
    return lax.ppermute(block, "wide", pairs(move))


def swap(block):
    return lax.ppermute(block, "narrow", [(0, 1), (1, 0)])


def project_kernel(now_ref, before_ref, small_ref, raise_ref, blend_ref, *refs):
    weights, out_ref, total_ref = refs[:8], refs[8], refs[9]
    step = pl.program_id(0)
    rank = raise_ref.shape[1]
    tile = 256
    for start in range(0, now_ref.shape[0], tile):
        rows = slice(start, start + tile)
        now = now_ref[rows, :].astype(F32)
        shift = before_ref[rows, :].astype(F32) - now
        for kind in range(4):
            low = jnp.dot(
                small_ref[rows, kind * rank : (kind + 1) * rank],
                raise_ref[kind],
                preferred_element_type=F32,
            )
            mixed = (now + shift * (blend_ref[kind : kind + 1, :] + low)).astype(BF16)
            for side in range(2):
                term = jnp.dot(mixed, weights[2 * kind + side][...], preferred_element_type=F32)
                slot = 2 * kind + side

                @pl.when(step == 0)
                def _():
                    total_ref[slot, rows, :] = term

                @pl.when(step > 0)
                def _():
                    total_ref[slot, rows, :] += term

    @pl.when(step == pl.num_programs(0) - 1)
    def _():
        out_ref[...] = total_ref[...].astype(BF16)


def project(now, before, small, raising, blending, weights):
    rows, features = now.shape
    columns = weights[0].shape[1]
    depth = 512
    return pl.pallas_call(
        project_kernel,
        grid=(features // depth,),
        in_specs=[
            pl.BlockSpec((rows, depth), lambda k: (0, k)),
            pl.BlockSpec((rows, depth), lambda k: (0, k)),
            pl.BlockSpec(small.shape, lambda k: (0, 0)),
            pl.BlockSpec((4, raising.shape[1], depth), lambda k: (0, 0, k)),
            pl.BlockSpec((4, depth), lambda k: (0, k)),
        ]
        + [pl.BlockSpec((depth, columns), lambda k: (k, 0))] * 8,
        out_specs=pl.BlockSpec((8, rows, columns), lambda k: (0, 0, 0)),
        out_shape=jax.ShapeDtypeStruct((8, rows, columns), BF16),
        scratch_shapes=[pltpu.VMEM((8, rows, columns), F32)],
        compiler_params=pltpu.CompilerParams(vmem_limit_bytes=48 * 2**20),
        cost_estimate=pl.CostEstimate(
            flops=2 * rows * features * columns * 8 + 8 * rows * features * 32,
            bytes_accessed=16 * features * columns + 4 * rows * features + 16 * rows * columns,
            transcendentals=0,
        ),
        name="project",
    )(now, before, small, raising, blending, *weights)


def recall_kernel(steps, *refs):
    state_ref, line_refs, refs = refs[0], refs[1 : 2 + steps], refs[2 + steps :]
    decay_ref, bonus_ref, gain_ref, offset_ref, out_ref, reach_ref, total_ref = refs
    part = pl.program_id(1)
    depth = state_ref.shape[1]
    span = state_ref.shape[2]
    width = state_ref.shape[3]
    now_ref = line_refs[steps]

    @pl.when(part == 0)
    def _():
        reach = now_ref[0]
        for step in range(steps):
            reach = reach * decay_ref[step]
        reach_ref[...] = reach
        total_ref[...] = jnp.zeros_like(total_ref)

    for start in range(0, width, 128):
        lanes = slice(start, start + 128)
        total = total_ref[:, lanes]
        reach = reach_ref[pl.ds(pl.multiple_of(part * depth, depth), depth), lanes]
        for row in range(depth):
            total = total + reach[row : row + 1, :] * state_ref[0, row, :, lanes]
        total_ref[:, lanes] = total

    @pl.when(part == pl.num_programs(1) - 1)
    def _():
        acceptor = now_ref[0]
        readout = total_ref[...]
        weight = jnp.sum(acceptor * bonus_ref[...] * now_ref[1], 0, keepdims=True)
        readout = readout + weight * now_ref[2]
        for step in reversed(range(steps)):
            weight = jnp.sum(acceptor * line_refs[step][1], 0, keepdims=True)
            readout = readout + weight * line_refs[step][2]
            if step:
                acceptor = acceptor * decay_ref[step]
        center = jnp.sum(readout, 0, keepdims=True) * (1.0 / span)
        offset = readout - center
        spread = jnp.sum(offset * offset, 0, keepdims=True) * (1.0 / span)
        scaled = offset * lax.rsqrt(spread + 0.00064)
        gate = now_ref[3]
        grouped = scaled * gain_ref[...] + offset_ref[...]
        out_ref[...] = (grouped * (gate / (1.0 + jnp.exp(-gate)))).astype(BF16)


def recall(state, lines, decay, bonus, gain, offset):
    heads, span, _, width = state.shape
    steps = len(lines) - 1
    depth = 16
    column = pl.BlockSpec((span, 1), lambda h, p: (h, 0))
    return pl.pallas_call(
        functools.partial(recall_kernel, steps),
        grid=(heads, span // depth),
        in_specs=[pl.BlockSpec((1, depth, span, width), lambda h, p: (h, p, 0, 0))]
        + [pl.BlockSpec((4, span, width), lambda h, p: (0, h, 0))] * (steps + 1)
        + [pl.BlockSpec((4, span, width), lambda h, p: (0, h, 0))]
        + [column] * 3,
        out_specs=pl.BlockSpec((span, width), lambda h, p: (h, 0)),
        out_shape=jax.ShapeDtypeStruct((heads * span, width), BF16),
        scratch_shapes=[pltpu.VMEM((span, width), F32), pltpu.VMEM((span, width), F32)],
        compiler_params=pltpu.CompilerParams(vmem_limit_bytes=32 * 2**20),
        cost_estimate=pl.CostEstimate(
            flops=2 * heads * span * span * width,
            bytes_accessed=4 * heads * span * span * width,
            transcendentals=heads * span * width,
        ),
        name="recall",
    )(state, *lines, decay, bonus, gain, offset)


def renew_kernel(state_ref, *refs):
    line_refs, decay_ref, out_ref, keep_ref, key_ref = refs[:-4], *refs[-4:]
    steps = len(line_refs)
    part = pl.program_id(1)
    depth = state_ref.shape[1]
    width = state_ref.shape[3]

    @pl.when(part == 0)
    def _():
        keep = jnp.ones_like(keep_ref)
        for step in reversed(range(steps)):
            key_ref[step] = line_refs[step][1] * keep
            keep = keep * decay_ref[step]
        keep_ref[...] = keep

    for start in range(0, width, 128):
        lanes = slice(start, start + 128)
        rows = pl.ds(pl.multiple_of(part * depth, depth), depth)
        keep = keep_ref[rows, lanes]
        keys = [key_ref[step, rows, lanes] for step in range(steps)]
        values = [line_refs[step][2, :, lanes] for step in range(steps)]
        for row in range(depth):
            here = slice(row, row + 1)
            total = keep[here] * state_ref[0, row, :, lanes]
            for step in range(steps):
                total = total + keys[step][here] * values[step]
            out_ref[0, row, :, lanes] = total


def renew(state, lines, decay):
    heads, span, _, width = state.shape
    depth = 16
    steps = len(lines)
    block = pl.BlockSpec((1, depth, span, width), lambda h, p: (h, p, 0, 0))
    return pl.pallas_call(
        renew_kernel,
        grid=(heads, span // depth),
        in_specs=[block] + [pl.BlockSpec((4, span, width), lambda h, p: (0, h, 0))] * (steps + 1),
        out_specs=block,
        out_shape=jax.ShapeDtypeStruct(state.shape, F32),
        scratch_shapes=[pltpu.VMEM((span, width), F32), pltpu.VMEM((steps, span, width), F32)],
        compiler_params=pltpu.CompilerParams(vmem_limit_bytes=32 * 2**20),
        cost_estimate=pl.CostEstimate(
            flops=9 * heads * span * span * width,
            bytes_accessed=8 * heads * span * span * width,
            transcendentals=0,
        ),
        name="renew",
    )(state, *lines, decay)


def boxed_device(
    sublevel_symbol_entries,
    prior_symbol_memory,
    entry_scaling_multiplier,
    entry_scaling_offset,
    learned_blending,
    blending_lowering_coefficients,
    blending_raising_coefficients,
    fading_lowering_coefficients,
    fading_raising_coefficients,
    learned_fading,
    immediate_item_premium,
    acceptor_projection,
    lookup_projection,
    payload_projection,
    gating_projection,
    emission_projection,
    group_scaling_multiplier,
    group_scaling_offset,
    dialogue_group_memory,
):
    rank = blending_raising_coefficients.shape[1]
    chats, moves, features = sublevel_symbol_entries.shape
    narrow_rows = dialogue_group_memory.shape[1]
    local_width = emission_projection.shape[1]
    groups = local_width // CHANNEL_SPAN
    wide, narrow = lax.axis_index("wide"), lax.axis_index("narrow")
    z, y, x = wide // 4, (wide // 2) % 2, wide % 2
    weights = (acceptor_projection, lookup_projection, payload_projection, gating_projection)

    def in_order(bit, mine, theirs):
        first = bit == 0
        return [jnp.where(first, mine, theirs), jnp.where(first, theirs, mine)]

    def gather(block):
        near = jnp.stack(in_order(z % 2, block, send(block, z_mate)))
        across = send(near, z_middle)
        far = jnp.where((z == 1) | (z == 2), across, send(across, z_outward))
        near = jnp.stack(in_order(y, near, send(near, y_mate)), 1)
        far = jnp.stack(in_order(y, far, send(far, y_mate)), 1)
        both = jnp.stack(in_order(z // 2, near, far))
        return both.reshape((8 * block.shape[0],) + block.shape[1:])

    all_weights = []
    for weight in weights:
        all_weights += [weight, send(weight, x_mate)]

    prior_all = gather(prior_symbol_memory)
    floats = sublevel_symbol_entries.astype(F32).transpose(1, 0, 2)
    sums = jnp.stack([jnp.sum(floats, -1), jnp.sum(floats * floats, -1)])
    sums = sums + swap(sums)
    center = sums[0][..., None] / FEATURE_EXTENT
    spread = sums[1][..., None] / FEATURE_EXTENT - center * center
    normed = (
        (floats - center) * lax.rsqrt(spread + 1e-05) * entry_scaling_multiplier
        + entry_scaling_offset
    ).astype(BF16)
    normed_all = [gather(normed[step]) for step in range(moves)]

    previous = jnp.concatenate([prior_symbol_memory[None], normed[:-1]], 0)
    normed_float = normed.astype(F32)
    shifted = previous.astype(F32) - normed_float
    blended = (normed_float + shifted * learned_blending[0]).astype(BF16)
    partial_mix = jnp.einsum(
        "msd,dr->msr", blended, blending_lowering_coefficients, preferred_element_type=F32
    )
    hidden = jnp.tanh(partial_mix + swap(partial_mix)).astype(BF16)
    decay_shift = jnp.einsum(
        "msr,rd->msd",
        hidden[..., :rank],
        blending_raising_coefficients[0],
        preferred_element_type=F32,
    )
    decay_mix = (normed_float + shifted * (learned_blending[1] + decay_shift)).astype(BF16)
    partial_decay = jnp.einsum(
        "msd,dr->msr", decay_mix, fading_lowering_coefficients, preferred_element_type=F32
    )
    decay_hidden = jnp.tanh(partial_decay + swap(partial_decay)).astype(BF16)
    small = jnp.concatenate([hidden[..., rank:], decay_hidden], -1).transpose(1, 0, 2)
    small_width = small.shape[-1]
    small_all = gather(small.reshape(chats, moves * small_width))
    small_all = small_all.reshape(-1, moves, small_width)

    half = small_all.shape[0] // 2
    decay_mine = lax.dynamic_slice_in_dim(small_all[..., 4 * rank :], narrow * half, half, 0)
    decay_theirs = send(decay_mine, x_mate)

    def weave(mine, theirs):
        shape = mine.shape[:-2] + (-1, chats, mine.shape[-1])
        both = jnp.stack(in_order(x, mine.reshape(shape), theirs.reshape(shape)), -3)
        return both.reshape(mine.shape[:-2] + (narrow_rows, mine.shape[-1]))

    decay_rows = weave(decay_mine.transpose(1, 0, 2), decay_theirs.transpose(1, 0, 2))
    decay_log = learned_fading[:, None] + jnp.einsum(
        "rd,msr->mds", fading_raising_coefficients, decay_rows, preferred_element_type=F32
    )
    decay = jnp.exp(-jnp.exp(decay_log))

    plane = emission_projection.shape[0] // PLANES
    piece = plane // 2
    emission = []
    for shift in range(PLANES):
        start = ((z + PLANES - shift) % PLANES) * plane
        if shift == 0:
            emission.append(lax.dynamic_slice_in_dim(emission_projection, start, plane, 0))
        else:
            own = lax.dynamic_slice_in_dim(
                emission_projection, start + narrow * piece, piece, 0
            )
            own = send(own, z_shift(-shift))
            emission.append(jnp.concatenate(in_order(narrow, own, swap(own)), 0))
    emission = jnp.concatenate(emission, 1)
    emission = emission.reshape(2, 2, local_width, PLANES * local_width)
    emission = jnp.stack(in_order(y, emission[0], emission[1]))
    emission = jnp.stack(in_order(x, emission[:, 0], emission[:, 1]), 1)
    emission = emission.reshape(plane, PLANES * local_width)

    state = dialogue_group_memory.reshape(groups, CHANNEL_SPAN, CHANNEL_SPAN, narrow_rows)
    bonus = immediate_item_premium[:, None]
    gain = group_scaling_multiplier[:, None]
    offset = group_scaling_offset[:, None]
    lines, results = [], []
    for step in range(moves):
        before = normed_all[step - 1] if step else prior_all
        partial = project(
            normed_all[step],
            before,
            small_all[:, step, : 4 * rank],
            blending_raising_coefficients[1:],
            learned_blending[2:],
            all_weights,
        )
        kept = lax.dynamic_slice_in_dim(partial, narrow * half, half, 1)
        given = lax.dynamic_slice_in_dim(partial, (1 - narrow) * half, half, 1)
        whole = kept.astype(F32) + swap(given).astype(F32)
        whole = whole.reshape(4, 2, half, local_width)
        theirs = send(whole[:, 1].astype(BF16), x_mate)
        line = weave(whole[:, 0], theirs.astype(F32)).transpose(0, 2, 1)
        lines.append(line)
        gated = recall(state, lines, decay, bonus, gain, offset)
        gated = jnp.concatenate([gated, send(gated, x_mate)], 0)
        gated = jnp.concatenate([gated, send(gated, y_mate)], 0)
        product = jnp.einsum("cs,ce->se", gated, emission, preferred_element_type=F32)
        total = product[:, :local_width]
        for shift in range(1, PLANES):
            columns = product[:, shift * local_width : (shift + 1) * local_width]
            total = total + send(columns.astype(BF16), z_shift(shift)).astype(F32)
        results.append(total.astype(BF16))
    final = renew(state, lines, decay)
    return (
        jnp.stack(results, 1),
        final.reshape(groups * CHANNEL_SPAN * CHANNEL_SPAN, narrow_rows),
    )


def solution(mesh):
    placed = (
        P("wide", None, "narrow"),
        P("wide", "narrow"),
        P("narrow"),
        P("narrow"),
        P(None, "narrow"),
        P("narrow", None),
        P(None, None, "narrow"),
        P("narrow", None),
        P(None, "wide"),
        P("wide"),
        P("wide"),
        P("narrow", "wide"),
        P("narrow", "wide"),
        P("narrow", "wide"),
        P("narrow", "wide"),
        P(None, "wide"),
        P("wide"),
        P("wide"),
        P("wide", "narrow"),
    )
    boxed = mesh.shape["wide"] == PLANES * 4 and mesh.shape["narrow"] == 2
    body = boxed_device if boxed else plain_device
    return jax.shard_map(
        body,
        mesh=mesh,
        in_specs=placed,
        out_specs=(P("narrow", None, "wide"), P("wide", "narrow")),
        check_vma=False,
    )
```

```python
import functools
import jax
import jax.numpy as jnp
from jax import lax
from jax.experimental import pallas as pl
from jax.experimental.pallas import tpu as pltpu
from jax.sharding import PartitionSpec as P

CHANNEL_SPAN = 64
FEATURE_EXTENT = 4096


def plain_device(
    sublevel_symbol_entries,
    prior_symbol_memory,
    entry_scaling_multiplier,
    entry_scaling_offset,
    learned_blending,
    blending_lowering_coefficients,
    blending_raising_coefficients,
    fading_lowering_coefficients,
    fading_raising_coefficients,
    learned_fading,
    immediate_item_premium,
    acceptor_projection,
    lookup_projection,
    payload_projection,
    gating_projection,
    emission_projection,
    group_scaling_multiplier,
    group_scaling_offset,
    dialogue_group_memory,
):
    rank = blending_raising_coefficients.shape[1]
    narrow_rows = dialogue_group_memory.shape[1]
    local_width = emission_projection.shape[1]
    group_partition = local_width // CHANNEL_SPAN
    weights = (acceptor_projection, lookup_projection, payload_projection, gating_projection)
    shift_gathered = lax.all_gather(prior_symbol_memory, "wide", axis=0, tiled=True)

    def channel_set_first(block):
        return block.reshape(narrow_rows, group_partition, CHANNEL_SPAN).transpose(1, 2, 0)

    present_symbol = dialogue_group_memory.reshape(
        group_partition, CHANNEL_SPAN, CHANNEL_SPAN, narrow_rows
    )
    previous_rows = prior_symbol_memory
    previous_all = shift_gathered
    results = []
    for index in range(sublevel_symbol_entries.shape[1]):
        floats = sublevel_symbol_entries[:, index : index + 1].astype(jnp.float32)
        totals, squares = lax.psum((jnp.sum(floats, -1), jnp.sum(floats * floats, -1)), "narrow")
        prepare_center = totals[..., None] / FEATURE_EXTENT
        spread = squares[..., None] / FEATURE_EXTENT - prepare_center * prepare_center
        normed = (
            (floats - prepare_center) * lax.rsqrt(spread + 1e-05) * entry_scaling_multiplier
            + entry_scaling_offset
        ).astype(jnp.bfloat16)
        previous = jnp.concatenate([previous_rows[:, None], normed[:, :-1]], 1)
        prepare_normalized_float = normed.astype(jnp.float32)
        prepare_shifted_input = previous.astype(jnp.float32) - prepare_normalized_float
        blended = (prepare_normalized_float + prepare_shifted_input * learned_blending[0]).astype(
            jnp.bfloat16
        )
        partial_mix = jnp.einsum(
            "smd,dr->smr",
            blended,
            blending_lowering_coefficients,
            preferred_element_type=jnp.float32,
        )
        hidden_activation = jnp.tanh(lax.psum(partial_mix, "narrow")).astype(jnp.bfloat16)
        decay_shift = jnp.einsum(
            "smr,rd->smd",
            hidden_activation[..., :rank],
            blending_raising_coefficients[0],
            preferred_element_type=jnp.float32,
        )
        decay_mix = (
            prepare_normalized_float + prepare_shifted_input * (learned_blending[1] + decay_shift)
        ).astype(jnp.bfloat16)
        partial_decay = jnp.einsum(
            "smd,dr->smr",
            decay_mix,
            fading_lowering_coefficients,
            preferred_element_type=jnp.float32,
        )
        decay_hidden = jnp.tanh(lax.psum(partial_decay, "narrow")).astype(jnp.bfloat16)
        small = jnp.concatenate([hidden_activation[..., rank:], decay_hidden], -1)
        prepare_normed_all = lax.all_gather(normed, "wide", axis=0, tiled=True)
        prepare_small_all = lax.all_gather(small, "wide", axis=0, tiled=True)
        normed, normed_all, small_all = (normed, prepare_normed_all, prepare_small_all)
        project_previous_all = previous_all[:, None]
        normalized_float = normed_all.astype(jnp.float32)
        shifted_input = project_previous_all.astype(jnp.float32) - normalized_float
        term_results = []
        for selector_index in range(4):
            low_rank_update = jnp.einsum(
                "smr,rd->smd",
                small_all[..., selector_index * rank : (selector_index + 1) * rank],
                blending_raising_coefficients[selector_index + 1],
                preferred_element_type=jnp.float32,
            )
            mixed_input = (
                normalized_float
                + shifted_input * (learned_blending[selector_index + 2] + low_rank_update)
            ).astype(jnp.bfloat16)
            term_results.append(
                jnp.einsum(
                    "smd,de->sme",
                    mixed_input,
                    weights[selector_index],
                    preferred_element_type=jnp.float32,
                )
            )
        project_transformed_outcome = lax.psum_scatter(
            jnp.concatenate(term_results, -1).astype(jnp.bfloat16),
            "narrow",
            scatter_dimension=0,
            tiled=True,
        ).astype(jnp.float32)
        rows_start = lax.axis_index("narrow") * narrow_rows
        decay_rows = lax.dynamic_slice_in_dim(
            small_all[..., 4 * rank :], rows_start, narrow_rows, 0
        )
        decay_log = learned_fading + jnp.einsum(
            "smr,rd->smd",
            decay_rows,
            fading_raising_coefficients,
            preferred_element_type=jnp.float32,
        )
        shrink_coefficient = jnp.exp(-jnp.exp(decay_log))
        recurrence_present_symbol = present_symbol
        each_group_reward = immediate_item_premium.reshape(group_partition, CHANNEL_SPAN)
        present_acceptor = channel_set_first(project_transformed_outcome[:, 0, :local_width])
        key_now = channel_set_first(
            project_transformed_outcome[:, 0, local_width : 2 * local_width]
        )
        value_now = channel_set_first(
            project_transformed_outcome[:, 0, 2 * local_width : 3 * local_width]
        )
        gate_now = project_transformed_outcome[:, 0, 3 * local_width :]
        forget_now = channel_set_first(shrink_coefficient[:, 0])
        dyadic_tensor = key_now[:, :, None, :] * value_now[:, None, :, :]
        memory_retrieval = jnp.sum(
            present_acceptor[:, :, None, :]
            * (recurrence_present_symbol + each_group_reward[:, :, None, None] * dyadic_tensor),
            1,
        )
        recurrence_present_symbol = (
            forget_now[:, :, None, :] * recurrence_present_symbol + dyadic_tensor
        )
        center = jnp.mean(memory_retrieval, 1, keepdims=True)
        offset = memory_retrieval - center
        scaled = offset * lax.rsqrt(jnp.mean(offset * offset, 1, keepdims=True) + 0.00064)
        squashed_vector = scaled.transpose(2, 0, 1).reshape(narrow_rows, local_width)
        pieces = [
            (
                (squashed_vector * group_scaling_multiplier + group_scaling_offset)
                * jax.nn.silu(gate_now)
            ).astype(jnp.bfloat16)
        ]
        present_symbol = recurrence_present_symbol
        gated = jnp.stack(pieces, 1)
        results.append(
            jnp.einsum(
                "smc,ce->sme",
                lax.all_gather(gated, "wide", axis=2, tiled=True),
                emission_projection,
                preferred_element_type=jnp.float32,
            ).astype(jnp.bfloat16)
        )
        previous_rows = normed[:, 0]
        previous_all = normed_all[:, 0]
    mixing_output = jnp.concatenate(results, 1)
    return (
        mixing_output,
        present_symbol.reshape(group_partition * CHANNEL_SPAN * CHANNEL_SPAN, narrow_rows),
    )


PLANES = 4
F32 = jnp.float32
BF16 = jnp.bfloat16


def pairs(move):
    moved = [(here, move(here)) for here in range(4 * PLANES)]
    return [(here, there) for here, there in moved if there is not None]


def x_mate(here):
    return here ^ 1


def y_mate(here):
    return here ^ 2


def z_shift(amount):
    return lambda here: (here + 4 * amount) % (4 * PLANES)


def send(block, move):
    return lax.ppermute(block, "wide", pairs(move))


def swap(block):
    return lax.ppermute(block, "narrow", [(0, 1), (1, 0)])


def project_kernel(order_ref, *refs):
    nows, befores, refs = refs[:8], refs[8:16], refs[16:]
    small_ref, raise_ref, blend_ref, own_ref, mate_ref, *refs = refs
    kept_refs, given_ref, now_ref, shift_ref, mix_ref = refs[:2], *refs[2:]
    rows = nows[0].shape[0]
    half, features = given_ref.shape[2], now_ref.shape[1]
    first = order_ref[8] == 0

    @pl.when(pl.program_id(0) == 0)
    def _():
        for block in range(8):
            here = pl.ds(pl.multiple_of(order_ref[block] * rows, rows), rows)
            now = nows[block][...]
            now_ref[here, :] = now
            shift_ref[here, :] = befores[block][...].astype(F32) - now.astype(F32)

    for start in range(0, features, 512):
        here = slice(start, start + 512)
        low = jnp.dot(small_ref[...], raise_ref[0, :, here], preferred_element_type=F32)
        mixed = now_ref[:, here].astype(F32) + shift_ref[:, here] * (blend_ref[0, :, here] + low)
        mix_ref[:, here] = mixed.astype(BF16)
    for side, weight_ref in enumerate((own_ref, mate_ref)):
        total = jnp.dot(mix_ref[...], weight_ref[0], preferred_element_type=F32).astype(BF16)
        kept_refs[side][0] = jnp.where(first, total[:half], total[half:])
        given_ref[side, 0] = jnp.where(first, total[half:], total[:half])


def project(order, nows, befores, small, raising, blending, own, mate):
    columns, features = own.shape[2], own.shape[1]
    rows = nows[0][0].shape[-2]
    total = 8 * rows

    def spec(source):
        array, place, column = source
        if place is None:
            return pl.BlockSpec((rows, features), lambda c, order: (0, column))
        return pl.BlockSpec((None, rows, features), lambda c, order: (place, 0, column))

    kind = lambda shape: pl.BlockSpec((1,) + shape[1:], lambda c, order: (c, 0, 0))
    sources = list(nows) + list(befores)
    return pl.pallas_call(
        project_kernel,
        grid_spec=pltpu.PrefetchScalarGridSpec(
            num_scalar_prefetch=1,
            grid=(4,),
            in_specs=[spec(source) for source in sources]
            + [pl.BlockSpec(small.shape, lambda c, order: (0, 0))]
            + [kind(raising.shape), kind(blending.shape), kind(own.shape), kind(mate.shape)],
            out_specs=[pl.BlockSpec((1, total // 2, columns), lambda c, order: (c, 0, 0))] * 2
            + [pl.BlockSpec((2, 1, total // 2, columns), lambda c, order: (0, c, 0, 0))],
            scratch_shapes=[
                pltpu.VMEM((total, features), BF16),
                pltpu.VMEM((total, features), F32),
                pltpu.VMEM((total, features), BF16),
            ],
        ),
        out_shape=[jax.ShapeDtypeStruct((4, total // 2, columns), BF16)] * 2
        + [jax.ShapeDtypeStruct((2, 4, total // 2, columns), BF16)],
        compiler_params=pltpu.CompilerParams(vmem_limit_bytes=48 * 2**20),
        cost_estimate=pl.CostEstimate(
            flops=2 * total * features * columns * 12,
            bytes_accessed=16 * features * columns + 4 * total * features,
            transcendentals=0,
        ),
        name="project",
    )(order, *[source[0] for source in sources], small, raising, blending, own, mate)


def weave_kernel(x_ref, kept_ref, given_ref, mate_ref, out_ref):
    chats = mate_ref.shape[1] // 4
    own = kept_ref[0].astype(F32) + given_ref[0, 0].astype(F32)
    mate = mate_ref[0].astype(F32)
    first = x_ref[0] == 0
    for block in range(4):
        rows = slice(block * chats, (block + 1) * chats)
        low = jnp.where(first, own[rows], mate[rows])
        high = jnp.where(first, mate[rows], own[rows])
        lanes = slice(2 * block * chats, 2 * (block + 1) * chats)
        out_ref[0, :, lanes] = jnp.concatenate([low, high], 0).T


def weave(x, kept, given, mate):
    _, half, columns = kept.shape
    side = pl.BlockSpec((1, half, columns), lambda c, x: (c, 0, 0))
    return pl.pallas_call(
        weave_kernel,
        grid_spec=pltpu.PrefetchScalarGridSpec(
            num_scalar_prefetch=1,
            grid=(4,),
            in_specs=[side, pl.BlockSpec((1, 1, half, columns), lambda c, x: (0, c, 0, 0)), side],
            out_specs=pl.BlockSpec((1, columns, 2 * half), lambda c, x: (c, 0, 0)),
        ),
        out_shape=jax.ShapeDtypeStruct((4, columns, 2 * half), F32),
        cost_estimate=pl.CostEstimate(
            flops=8 * half * columns, bytes_accessed=64 * half * columns, transcendentals=0
        ),
        name="weave",
    )(x, kept, given, mate)


def recall_kernel(steps, *refs):
    last = steps[-1]
    state_ref, line_refs, refs = refs[0], refs[1 : 2 + last], refs[2 + last :]
    decay_ref, bonus_ref, gain_ref, offset_ref = refs[:4]
    out_refs, (reach_ref, total_ref) = refs[4:-2], refs[-2:]
    part = pl.program_id(1)
    depth = state_ref.shape[1]
    span = state_ref.shape[2]
    width = state_ref.shape[3]

    @pl.when(part == 0)
    def _():
        for slot, step in enumerate(steps):
            reach = line_refs[step][0]
            for earlier in range(step):
                reach = reach * decay_ref[earlier]
            reach_ref[slot] = reach
        total_ref[...] = jnp.zeros_like(total_ref)

    for start in range(0, width, 128):
        lanes = slice(start, start + 128)
        here = pl.ds(pl.multiple_of(part * depth, depth), depth)
        totals = [total_ref[slot, :, lanes] for slot in range(len(steps))]
        reaches = [reach_ref[slot, here, lanes] for slot in range(len(steps))]
        for row in range(depth):
            memory = state_ref[0, row, :, lanes]
            for slot in range(len(steps)):
                totals[slot] = totals[slot] + reaches[slot][row : row + 1, :] * memory
        for slot in range(len(steps)):
            total_ref[slot, :, lanes] = totals[slot]

    @pl.when(part == pl.num_programs(1) - 1)
    def _():
        for slot, step in enumerate(steps):
            now_ref = line_refs[step]
            acceptor = now_ref[0]
            readout = total_ref[slot]
            weight = jnp.sum(acceptor * bonus_ref[...] * now_ref[1], 0, keepdims=True)
            readout = readout + weight * now_ref[2]
            for earlier in reversed(range(step)):
                weight = jnp.sum(acceptor * line_refs[earlier][1], 0, keepdims=True)
                readout = readout + weight * line_refs[earlier][2]
                if earlier:
                    acceptor = acceptor * decay_ref[earlier]
            center = jnp.sum(readout, 0, keepdims=True) * (1.0 / span)
            offset = readout - center
            spread = jnp.sum(offset * offset, 0, keepdims=True) * (1.0 / span)
            scaled = offset * lax.rsqrt(spread + 0.00064)
            gate = now_ref[3]
            grouped = scaled * gain_ref[...] + offset_ref[...]
            out_refs[slot][...] = (grouped * (gate / (1.0 + jnp.exp(-gate)))).astype(BF16)


def recall(state, steps, lines, decay, bonus, gain, offset):
    heads, span, _, width = state.shape
    depth = span // 2
    column = pl.BlockSpec((span, 1), lambda h, p: (h, 0))
    return pl.pallas_call(
        functools.partial(recall_kernel, steps),
        grid=(heads, span // depth),
        in_specs=[pl.BlockSpec((1, depth, span, width), lambda h, p: (h, p, 0, 0))]
        + [pl.BlockSpec((4, span, width), lambda h, p: (0, h, 0))] * len(lines)
        + [pl.BlockSpec((decay.shape[0], span, width), lambda h, p: (0, h, 0))]
        + [column] * 3,
        out_specs=[pl.BlockSpec((span, width), lambda h, p: (h, 0))] * len(steps),
        out_shape=[jax.ShapeDtypeStruct((heads * span, width), BF16)] * len(steps),
        scratch_shapes=[pltpu.VMEM((len(steps), span, width), F32)] * 2,
        compiler_params=pltpu.CompilerParams(vmem_limit_bytes=60 * 2**20),
        cost_estimate=pl.CostEstimate(
            flops=2 * heads * span * span * width,
            bytes_accessed=4 * heads * span * span * width,
            transcendentals=heads * span * width,
        ),
        name="recall",
    )(state, *lines, decay, bonus, gain, offset)


def renew_kernel(state_ref, *refs):
    line_refs, decay_ref, out_ref, keep_ref, key_ref = refs[:-4], *refs[-4:]
    steps = len(line_refs)
    part = pl.program_id(1)
    depth = state_ref.shape[1]
    width = state_ref.shape[3]

    @pl.when(part == 0)
    def _():
        keep = jnp.ones_like(keep_ref)
        for step in reversed(range(steps)):
            key_ref[step] = line_refs[step][1] * keep
            keep = keep * decay_ref[step]
        keep_ref[...] = keep

    for start in range(0, width, 128):
        lanes = slice(start, start + 128)
        rows = pl.ds(pl.multiple_of(part * depth, depth), depth)
        keep = keep_ref[rows, lanes]
        keys = [key_ref[step, rows, lanes] for step in range(steps)]
        values = [line_refs[step][2, :, lanes] for step in range(steps)]
        for row in range(depth):
            here = slice(row, row + 1)
            total = keep[here] * state_ref[0, row, :, lanes]
            for step in range(steps):
                total = total + keys[step][here] * values[step]
            out_ref[0, row, :, lanes] = total


def renew(state, lines, decay):
    heads, span, _, width = state.shape
    depth = span // 2
    steps = len(lines)
    block = pl.BlockSpec((1, depth, span, width), lambda h, p: (h, p, 0, 0))
    return pl.pallas_call(
        renew_kernel,
        grid=(heads, span // depth),
        in_specs=[block] + [pl.BlockSpec((4, span, width), lambda h, p: (0, h, 0))] * (steps + 1),
        out_specs=block,
        out_shape=jax.ShapeDtypeStruct(state.shape, F32),
        scratch_shapes=[pltpu.VMEM((span, width), F32), pltpu.VMEM((steps, span, width), F32)],
        compiler_params=pltpu.CompilerParams(vmem_limit_bytes=40 * 2**20),
        cost_estimate=pl.CostEstimate(
            flops=9 * heads * span * span * width,
            bytes_accessed=8 * heads * span * span * width,
            transcendentals=0,
        ),
        name="renew",
    )(state, *lines, decay)


def boxed_device(
    sublevel_symbol_entries,
    prior_symbol_memory,
    entry_scaling_multiplier,
    entry_scaling_offset,
    learned_blending,
    blending_lowering_coefficients,
    blending_raising_coefficients,
    fading_lowering_coefficients,
    fading_raising_coefficients,
    learned_fading,
    immediate_item_premium,
    acceptor_projection,
    lookup_projection,
    payload_projection,
    gating_projection,
    emission_projection,
    group_scaling_multiplier,
    group_scaling_offset,
    dialogue_group_memory,
):
    rank = blending_raising_coefficients.shape[1]
    chats, moves, features = sublevel_symbol_entries.shape
    narrow_rows = dialogue_group_memory.shape[1]
    local_width = emission_projection.shape[1]
    groups = local_width // CHANNEL_SPAN
    wide, narrow = lax.axis_index("wide"), lax.axis_index("narrow")
    z, y, x = wide // 4, (wide // 2) % 2, wide % 2
    weights = (acceptor_projection, lookup_projection, payload_projection, gating_projection)

    def in_order(bit, mine, theirs):
        first = bit == 0
        return [jnp.where(first, mine, theirs), jnp.where(first, theirs, mine)]

    def after(value, *earlier):
        return lax.optimization_barrier((value, *earlier))[0]

    order = jnp.stack(
        [
            2 * ((z + PLANES - shift) % PLANES) + row
            for row in (y, 1 - y)
            for shift in range(PLANES)
        ]
        + [narrow]
    ).astype(jnp.int32)

    own_weights = jnp.stack(weights)
    mate_weights = send(own_weights, x_mate)

    def send_z(block, *earlier):
        return [
            send(after(block, *[one[shift - 1] for one in earlier]), z_shift(shift))
            for shift in range(1, PLANES)
        ]

    prior_z = send_z(prior_symbol_memory)

    floats = sublevel_symbol_entries.astype(F32).transpose(1, 0, 2)
    sums = jnp.stack([jnp.sum(floats, -1), jnp.sum(floats * floats, -1)])
    sums = sums + swap(sums)
    center = sums[0][..., None] / FEATURE_EXTENT
    spread = sums[1][..., None] / FEATURE_EXTENT - center * center
    normed = (
        (floats - center) * lax.rsqrt(spread + 1e-05) * entry_scaling_multiplier
        + entry_scaling_offset
    ).astype(BF16)
    previous = jnp.concatenate([prior_symbol_memory[None], normed[:-1]], 0)
    normed_float = normed.astype(F32)
    shifted = previous.astype(F32) - normed_float
    blended = (normed_float + shifted * learned_blending[0]).astype(BF16)
    partial_mix = jnp.einsum(
        "msd,dr->msr", blended, blending_lowering_coefficients, preferred_element_type=F32
    )
    hidden = jnp.tanh(partial_mix + swap(partial_mix)).astype(BF16)
    decay_shift = jnp.einsum(
        "msr,rd->msd",
        hidden[..., :rank],
        blending_raising_coefficients[0],
        preferred_element_type=F32,
    )
    decay_mix = (normed_float + shifted * (learned_blending[1] + decay_shift)).astype(BF16)
    partial_decay = jnp.einsum(
        "msd,dr->msr", decay_mix, fading_lowering_coefficients, preferred_element_type=F32
    )
    decay_hidden = jnp.tanh(partial_decay + swap(partial_decay)).astype(BF16)

    small = jnp.concatenate(
        [hidden[step, :, rank:] for step in range(moves)]
        + [decay_hidden[step] for step in range(moves)],
        1,
    )
    def in_plane(passed):
        passed = jnp.stack((passed[:1] + passed[:0:-1]) * 2)
        return lax.dynamic_slice_in_dim(passed, (PLANES - z) % PLANES, PLANES, 0)

    first = jnp.concatenate([normed[0], normed[1]], 1)
    second = jnp.concatenate([normed[2], normed[3]], 1)
    normed_y = send(jnp.stack([first, second]), y_mate)
    small_z = send_z(small, prior_z)
    prior_y = send(jnp.stack([prior_symbol_memory] + prior_z), y_mate)
    first_z = send_z(first, small_z)
    small_plane = in_plane([small] + small_z)
    small_y = send(small_plane, y_mate)
    first_near_y = send(after(first_z[0], normed_y), y_mate)
    second_z = send_z(second, first_z, (prior_y, small_y, first_near_y))
    first_far_y = send(jnp.stack(first_z[1:]), y_mate)
    second_near_y = send(after(second_z[0], first_near_y), y_mate)
    small_all = jnp.stack(in_order(y, small_plane, small_y), 1).reshape(-1, small.shape[1])

    prior_sources = [(prior_symbol_memory, None, 0)] + [(one, None, 0) for one in prior_z]
    prior_sources += [(prior_y, place, 0) for place in range(PLANES)]

    def first_sources(step):
        found = [(first, None, step)] + [(one, None, step) for one in first_z]
        found += [(normed_y, 0, step), (first_near_y, None, step)]
        return found + [(first_far_y, place, step) for place in range(2)]

    half = small_all.shape[0] // 2
    decay_width = decay_hidden.shape[-1]
    decay_own = lax.dynamic_slice_in_dim(small_all[:, moves * 4 * rank :], narrow * half, half, 0)
    decay_rows = jnp.stack(
        in_order(x, decay_own.reshape(-1, chats, moves * decay_width),
                 send(decay_own, x_mate).reshape(-1, chats, moves * decay_width)),
        1,
    ).reshape(narrow_rows, moves, decay_width)
    decay_log = learned_fading[:, None] + jnp.einsum(
        "rd,smr->mds", fading_raising_coefficients, decay_rows, preferred_element_type=F32
    )
    decay = jnp.exp(-jnp.exp(decay_log))

    blocks = emission_projection.reshape(4 * PLANES, local_width, local_width)

    def plane_rows(shift, mates):
        start = ((z + PLANES - shift) % PLANES) * 4
        rows = [
            lax.dynamic_index_in_dim(blocks, start + (wide % 4 ^ mate), 0, False)
            for mate in mates
        ]
        return jnp.concatenate(rows, 0)

    emission_own = plane_rows(0, range(4))
    state = dialogue_group_memory.reshape(groups, CHANNEL_SPAN, CHANNEL_SPAN, narrow_rows)
    bonus = immediate_item_premium[:, None]
    gain = group_scaling_multiplier[:, None]
    offset = group_scaling_offset[:, None]
    raising = jnp.stack(
        [
            jnp.pad(blending_raising_coefficients[kind + 1], ((kind * rank, (3 - kind) * rank), (0, 0)))
            for kind in range(4)
        ]
    )
    blending = learned_blending[2:, None]
    x_here = x.astype(jnp.int32)[None]
    lines = []

    def make(step, nows, befores, *earlier):
        return project(
            after(order, *earlier),
            nows,
            befores,
            small_all[:, step * 4 * rank : (step + 1) * 4 * rank],
            raising,
            blending,
            own_weights,
            mate_weights,
        )

    def pass_on(made, *earlier):
        _, mate_kept, given = made
        theirs = after(mate_kept, *earlier).astype(F32) + given[1].astype(F32)
        theirs = theirs.astype(BF16)
        return theirs, send(theirs, x_mate)

    def line_up(made, arrived, *earlier):
        lines.append(weave(after(x_here, *earlier), made[0], made[2], arrived))
        return lines[-1]

    def read(step, *earlier):
        line = lines[: step + 1]
        gated = recall(state, (step,), line, decay, after(bonus, *earlier), gain, offset)[0]
        gated = jnp.concatenate([gated, send(gated, x_mate)], 0)
        return gated, jnp.concatenate([gated, send(gated, y_mate)], 0)

    def emit(gated, *earlier):
        gated = after(gated, *earlier)
        own = jnp.einsum("cs,ce->se", gated, emission_own, preferred_element_type=F32)
        far = jnp.einsum("cs,ce->se", gated, emission_far, preferred_element_type=F32)
        return own, far.astype(BF16)

    def gather_up(product, *earlier):
        total, far = product
        arrived = [
            send(far[:, shift * local_width : (shift + 1) * local_width], z_shift(shift + 1))
            for shift in range(PLANES - 1)
        ]
        if earlier:
            arrived = after(tuple(arrived), *earlier)
        for one in arrived:
            total = total + one.astype(F32)
        return total.astype(BF16)

    def halves(made):
        return made[0], made[1], swap(made[2])

    made = [halves(make(0, first_sources(0), prior_sources))]
    second_far_y = send(after(jnp.stack(second_z[1:]), made[0][0]), y_mate)

    def second_sources(step):
        found = [(second, None, step)] + [(one, None, step) for one in second_z]
        found += [(normed_y, 1, step), (second_near_y, None, step)]
        return found + [(second_far_y, place, step) for place in range(2)]

    made.append(halves(make(1, first_sources(1), first_sources(0), second_near_y, made[0][0])))
    passed = [pass_on(made[0], made[1][0])]
    emission_z = [
        send(
            after(plane_rows(shift, (2 * narrow, 2 * narrow + 1)), second_z[shift - 1], passed[0][0]),
            z_shift(-shift),
        )
        for shift in range(1, PLANES)
    ]
    passed.append(pass_on(made[1]))
    line_up(made[0], passed[0][1])
    gated = [read(0)]
    made.append(halves(make(2, second_sources(0), first_sources(1), gated[0][0])))
    line_up(made[1], passed[1][1], made[2][0])
    passed.append(pass_on(made[2], lines[1]))
    made.append(
        halves(make(3, second_sources(1), second_sources(0), lines[1], *emission_z))
    )
    emission_near = jnp.concatenate(emission_z, 1)
    emission_far = jnp.concatenate(in_order(narrow, emission_near, swap(emission_near)), 0)
    products = [emit(gated[0][1], made[3][0])]
    results = [gather_up(products[0])]
    passed.append(pass_on(made[3], products[0][1]))
    gated.append(read(1, products[0][1], passed[2][0], passed[3][0]))
    line_up(made[2], passed[2][1], gated[1][0])
    gated.append(read(2))
    line_up(made[3], passed[3][1], gated[2][0])
    products.append(emit(gated[1][1], lines[3]))
    gated.append(read(3, products[1][1], results[0]))
    products.append(emit(gated[2][1], gated[3][0]))
    products.append(emit(gated[3][1], products[2][1]))
    final = renew(after(state, products[3][1]), lines, decay)
    results += [gather_up(products[1]), gather_up(products[2])]
    results.append(gather_up(products[3], final))
    return (
        jnp.stack(results, 1),
        final.reshape(groups * CHANNEL_SPAN * CHANNEL_SPAN, narrow_rows),
    )


def solution(mesh):
    placed = (
        P("wide", None, "narrow"),
        P("wide", "narrow"),
        P("narrow"),
        P("narrow"),
        P(None, "narrow"),
        P("narrow", None),
        P(None, None, "narrow"),
        P("narrow", None),
        P(None, "wide"),
        P("wide"),
        P("wide"),
        P("narrow", "wide"),
        P("narrow", "wide"),
        P("narrow", "wide"),
        P("narrow", "wide"),
        P(None, "wide"),
        P("wide"),
        P("wide"),
        P("wide", "narrow"),
    )
    boxed = mesh.shape["wide"] == PLANES * 4 and mesh.shape["narrow"] == 2
    body = boxed_device if boxed else plain_device
    return jax.shard_map(
        body,
        mesh=mesh,
        in_specs=placed,
        out_specs=(P("narrow", None, "wide"), P("wide", "narrow")),
        check_vma=False,
    )
```

```python
import functools
import jax
import jax.numpy as jnp
from jax import lax
from jax.experimental import pallas as pl
from jax.experimental.pallas import tpu as pltpu
from jax.sharding import PartitionSpec as P

CHANNEL_SPAN = 64
FEATURE_EXTENT = 4096


def plain_device(
    sublevel_symbol_entries,
    prior_symbol_memory,
    entry_scaling_multiplier,
    entry_scaling_offset,
    learned_blending,
    blending_lowering_coefficients,
    blending_raising_coefficients,
    fading_lowering_coefficients,
    fading_raising_coefficients,
    learned_fading,
    immediate_item_premium,
    acceptor_projection,
    lookup_projection,
    payload_projection,
    gating_projection,
    emission_projection,
    group_scaling_multiplier,
    group_scaling_offset,
    dialogue_group_memory,
):
    rank = blending_raising_coefficients.shape[1]
    narrow_rows = dialogue_group_memory.shape[1]
    local_width = emission_projection.shape[1]
    group_partition = local_width // CHANNEL_SPAN
    weights = (acceptor_projection, lookup_projection, payload_projection, gating_projection)
    shift_gathered = lax.all_gather(prior_symbol_memory, "wide", axis=0, tiled=True)

    def channel_set_first(block):
        return block.reshape(narrow_rows, group_partition, CHANNEL_SPAN).transpose(1, 2, 0)

    present_symbol = dialogue_group_memory.reshape(
        group_partition, CHANNEL_SPAN, CHANNEL_SPAN, narrow_rows
    )
    previous_rows = prior_symbol_memory
    previous_all = shift_gathered
    results = []
    for index in range(sublevel_symbol_entries.shape[1]):
        floats = sublevel_symbol_entries[:, index : index + 1].astype(jnp.float32)
        totals, squares = lax.psum((jnp.sum(floats, -1), jnp.sum(floats * floats, -1)), "narrow")
        prepare_center = totals[..., None] / FEATURE_EXTENT
        spread = squares[..., None] / FEATURE_EXTENT - prepare_center * prepare_center
        normed = (
            (floats - prepare_center) * lax.rsqrt(spread + 1e-05) * entry_scaling_multiplier
            + entry_scaling_offset
        ).astype(jnp.bfloat16)
        previous = jnp.concatenate([previous_rows[:, None], normed[:, :-1]], 1)
        prepare_normalized_float = normed.astype(jnp.float32)
        prepare_shifted_input = previous.astype(jnp.float32) - prepare_normalized_float
        blended = (prepare_normalized_float + prepare_shifted_input * learned_blending[0]).astype(
            jnp.bfloat16
        )
        partial_mix = jnp.einsum(
            "smd,dr->smr",
            blended,
            blending_lowering_coefficients,
            preferred_element_type=jnp.float32,
        )
        hidden_activation = jnp.tanh(lax.psum(partial_mix, "narrow")).astype(jnp.bfloat16)
        decay_shift = jnp.einsum(
            "smr,rd->smd",
            hidden_activation[..., :rank],
            blending_raising_coefficients[0],
            preferred_element_type=jnp.float32,
        )
        decay_mix = (
            prepare_normalized_float + prepare_shifted_input * (learned_blending[1] + decay_shift)
        ).astype(jnp.bfloat16)
        partial_decay = jnp.einsum(
            "smd,dr->smr",
            decay_mix,
            fading_lowering_coefficients,
            preferred_element_type=jnp.float32,
        )
        decay_hidden = jnp.tanh(lax.psum(partial_decay, "narrow")).astype(jnp.bfloat16)
        small = jnp.concatenate([hidden_activation[..., rank:], decay_hidden], -1)
        prepare_normed_all = lax.all_gather(normed, "wide", axis=0, tiled=True)
        prepare_small_all = lax.all_gather(small, "wide", axis=0, tiled=True)
        normed, normed_all, small_all = (normed, prepare_normed_all, prepare_small_all)
        project_previous_all = previous_all[:, None]
        normalized_float = normed_all.astype(jnp.float32)
        shifted_input = project_previous_all.astype(jnp.float32) - normalized_float
        term_results = []
        for selector_index in range(4):
            low_rank_update = jnp.einsum(
                "smr,rd->smd",
                small_all[..., selector_index * rank : (selector_index + 1) * rank],
                blending_raising_coefficients[selector_index + 1],
                preferred_element_type=jnp.float32,
            )
            mixed_input = (
                normalized_float
                + shifted_input * (learned_blending[selector_index + 2] + low_rank_update)
            ).astype(jnp.bfloat16)
            term_results.append(
                jnp.einsum(
                    "smd,de->sme",
                    mixed_input,
                    weights[selector_index],
                    preferred_element_type=jnp.float32,
                )
            )
        project_transformed_outcome = lax.psum_scatter(
            jnp.concatenate(term_results, -1).astype(jnp.bfloat16),
            "narrow",
            scatter_dimension=0,
            tiled=True,
        ).astype(jnp.float32)
        rows_start = lax.axis_index("narrow") * narrow_rows
        decay_rows = lax.dynamic_slice_in_dim(
            small_all[..., 4 * rank :], rows_start, narrow_rows, 0
        )
        decay_log = learned_fading + jnp.einsum(
            "smr,rd->smd",
            decay_rows,
            fading_raising_coefficients,
            preferred_element_type=jnp.float32,
        )
        shrink_coefficient = jnp.exp(-jnp.exp(decay_log))
        recurrence_present_symbol = present_symbol
        each_group_reward = immediate_item_premium.reshape(group_partition, CHANNEL_SPAN)
        present_acceptor = channel_set_first(project_transformed_outcome[:, 0, :local_width])
        key_now = channel_set_first(
            project_transformed_outcome[:, 0, local_width : 2 * local_width]
        )
        value_now = channel_set_first(
            project_transformed_outcome[:, 0, 2 * local_width : 3 * local_width]
        )
        gate_now = project_transformed_outcome[:, 0, 3 * local_width :]
        forget_now = channel_set_first(shrink_coefficient[:, 0])
        dyadic_tensor = key_now[:, :, None, :] * value_now[:, None, :, :]
        memory_retrieval = jnp.sum(
            present_acceptor[:, :, None, :]
            * (recurrence_present_symbol + each_group_reward[:, :, None, None] * dyadic_tensor),
            1,
        )
        recurrence_present_symbol = (
            forget_now[:, :, None, :] * recurrence_present_symbol + dyadic_tensor
        )
        center = jnp.mean(memory_retrieval, 1, keepdims=True)
        offset = memory_retrieval - center
        scaled = offset * lax.rsqrt(jnp.mean(offset * offset, 1, keepdims=True) + 0.00064)
        squashed_vector = scaled.transpose(2, 0, 1).reshape(narrow_rows, local_width)
        pieces = [
            (
                (squashed_vector * group_scaling_multiplier + group_scaling_offset)
                * jax.nn.silu(gate_now)
            ).astype(jnp.bfloat16)
        ]
        present_symbol = recurrence_present_symbol
        gated = jnp.stack(pieces, 1)
        results.append(
            jnp.einsum(
                "smc,ce->sme",
                lax.all_gather(gated, "wide", axis=2, tiled=True),
                emission_projection,
                preferred_element_type=jnp.float32,
            ).astype(jnp.bfloat16)
        )
        previous_rows = normed[:, 0]
        previous_all = normed_all[:, 0]
    mixing_output = jnp.concatenate(results, 1)
    return (
        mixing_output,
        present_symbol.reshape(group_partition * CHANNEL_SPAN * CHANNEL_SPAN, narrow_rows),
    )


PLANES = 4
F32 = jnp.float32
BF16 = jnp.bfloat16


def pairs(move):
    moved = [(here, move(here)) for here in range(4 * PLANES)]
    return [(here, there) for here, there in moved if there is not None]


def x_mate(here):
    return here ^ 1


def y_mate(here):
    return here ^ 2


def z_shift(amount):
    return lambda here: (here + 4 * amount) % (4 * PLANES)


def send(block, move):
    return lax.ppermute(block, "wide", pairs(move))


def swap(block):
    return lax.ppermute(block, "narrow", [(0, 1), (1, 0)])


def project_kernel(order_ref, *refs):
    nows, befores, refs = refs[:8], refs[8:16], refs[16:]
    small_ref, raise_ref, blend_ref, own_ref, mate_ref, *refs = refs
    kept_refs, given_ref, now_ref, shift_ref, mix_ref = refs[:2], *refs[2:]
    rows = nows[0].shape[0]
    half, features = given_ref.shape[2], now_ref.shape[1]
    first = order_ref[8] == 0

    @pl.when(pl.program_id(0) == 0)
    def _():
        for block in range(8):
            here = pl.ds(pl.multiple_of(order_ref[block] * rows, rows), rows)
            now = nows[block][...]
            now_ref[here, :] = now
            shift_ref[here, :] = befores[block][...].astype(F32) - now.astype(F32)

    for start in range(0, features, 512):
        here = slice(start, start + 512)
        low = jnp.dot(small_ref[...], raise_ref[0, :, here], preferred_element_type=F32)
        mixed = now_ref[:, here].astype(F32) + shift_ref[:, here] * (blend_ref[0, :, here] + low)
        mix_ref[:, here] = mixed.astype(BF16)
    for side, weight_ref in enumerate((own_ref, mate_ref)):
        total = jnp.dot(mix_ref[...], weight_ref[0], preferred_element_type=F32).astype(BF16)
        kept_refs[side][0] = jnp.where(first, total[:half], total[half:])
        given_ref[side, 0] = jnp.where(first, total[half:], total[:half])


def project(order, nows, befores, small, raising, blending, own, mate):
    columns, features = own.shape[2], own.shape[1]
    rows = nows[0][0].shape[-2]
    total = 8 * rows

    def spec(source):
        array, place, column = source
        if place is None:
            return pl.BlockSpec((rows, features), lambda c, order: (0, column))
        return pl.BlockSpec((None, rows, features), lambda c, order: (place, 0, column))

    kind = lambda shape: pl.BlockSpec((1,) + shape[1:], lambda c, order: (c, 0, 0))
    sources = list(nows) + list(befores)
    return pl.pallas_call(
        project_kernel,
        grid_spec=pltpu.PrefetchScalarGridSpec(
            num_scalar_prefetch=1,
            grid=(4,),
            in_specs=[spec(source) for source in sources]
            + [pl.BlockSpec(small.shape, lambda c, order: (0, 0))]
            + [kind(raising.shape), kind(blending.shape), kind(own.shape), kind(mate.shape)],
            out_specs=[pl.BlockSpec((1, total // 2, columns), lambda c, order: (c, 0, 0))] * 2
            + [pl.BlockSpec((2, 1, total // 2, columns), lambda c, order: (0, c, 0, 0))],
            scratch_shapes=[
                pltpu.VMEM((total, features), BF16),
                pltpu.VMEM((total, features), F32),
                pltpu.VMEM((total, features), BF16),
            ],
        ),
        out_shape=[jax.ShapeDtypeStruct((4, total // 2, columns), BF16)] * 2
        + [jax.ShapeDtypeStruct((2, 4, total // 2, columns), BF16)],
        compiler_params=pltpu.CompilerParams(vmem_limit_bytes=48 * 2**20),
        cost_estimate=pl.CostEstimate(
            flops=2 * total * features * columns * 12,
            bytes_accessed=16 * features * columns + 4 * total * features,
            transcendentals=0,
        ),
        name="project",
    )(order, *[source[0] for source in sources], small, raising, blending, own, mate)


def weave_kernel(x_ref, kept_ref, given_ref, mate_ref, out_ref):
    chats = mate_ref.shape[1] // 4
    own = (kept_ref[0].astype(F32) + given_ref[0, 0].astype(F32)).astype(BF16)
    mate = mate_ref[0]
    first = x_ref[0] == 0
    for block in range(4):
        rows = slice(block * chats, (block + 1) * chats)
        low = jnp.where(first, own[rows], mate[rows])
        high = jnp.where(first, mate[rows], own[rows])
        lanes = slice(2 * block * chats, 2 * (block + 1) * chats)
        out_ref[0, :, lanes] = jnp.concatenate([low, high], 0).T


def weave(x, kept, given, mate):
    _, half, columns = kept.shape
    side = pl.BlockSpec((1, half, columns), lambda c, x: (c, 0, 0))
    return pl.pallas_call(
        weave_kernel,
        grid_spec=pltpu.PrefetchScalarGridSpec(
            num_scalar_prefetch=1,
            grid=(4,),
            in_specs=[side, pl.BlockSpec((1, 1, half, columns), lambda c, x: (0, c, 0, 0)), side],
            out_specs=pl.BlockSpec((1, columns, 2 * half), lambda c, x: (c, 0, 0)),
        ),
        out_shape=jax.ShapeDtypeStruct((4, columns, 2 * half), BF16),
        cost_estimate=pl.CostEstimate(
            flops=8 * half * columns, bytes_accessed=64 * half * columns, transcendentals=0
        ),
        name="weave",
    )(x, kept, given, mate)


def recall_kernel(steps, *refs):
    last = steps[-1]
    state_ref, line_refs, refs = refs[0], refs[1 : 2 + last], refs[2 + last :]
    decay_ref, bonus_ref, gain_ref, offset_ref = refs[:4]
    out_refs, (reach_ref, total_ref) = refs[4:-2], refs[-2:]
    part = pl.program_id(1)
    depth = state_ref.shape[1]
    span = state_ref.shape[2]
    width = state_ref.shape[3]

    @pl.when(part == 0)
    def _():
        for slot, step in enumerate(steps):
            reach = line_refs[step][0].astype(F32)
            for earlier in range(step):
                reach = reach * decay_ref[earlier]
            reach_ref[slot] = reach
        total_ref[...] = jnp.zeros_like(total_ref)

    for start in range(0, width, 128):
        lanes = slice(start, start + 128)
        here = pl.ds(pl.multiple_of(part * depth, depth), depth)
        totals = [total_ref[slot, :, lanes] for slot in range(len(steps))]
        reaches = [reach_ref[slot, here, lanes] for slot in range(len(steps))]
        for row in range(depth):
            memory = state_ref[0, row, :, lanes]
            for slot in range(len(steps)):
                totals[slot] = totals[slot] + reaches[slot][row : row + 1, :] * memory
        for slot in range(len(steps)):
            total_ref[slot, :, lanes] = totals[slot]

    @pl.when(part == pl.num_programs(1) - 1)
    def _():
        for slot, step in enumerate(steps):
            now_ref = line_refs[step]
            acceptor = now_ref[0].astype(F32)
            readout = total_ref[slot]
            weight = jnp.sum(acceptor * bonus_ref[...] * now_ref[1].astype(F32), 0, keepdims=True)
            readout = readout + weight * now_ref[2].astype(F32)
            for earlier in reversed(range(step)):
                weight = jnp.sum(acceptor * line_refs[earlier][1].astype(F32), 0, keepdims=True)
                readout = readout + weight * line_refs[earlier][2].astype(F32)
                if earlier:
                    acceptor = acceptor * decay_ref[earlier]
            center = jnp.sum(readout, 0, keepdims=True) * (1.0 / span)
            offset = readout - center
            spread = jnp.sum(offset * offset, 0, keepdims=True) * (1.0 / span)
            scaled = offset * lax.rsqrt(spread + 0.00064)
            gate = now_ref[3].astype(F32)
            grouped = scaled * gain_ref[...] + offset_ref[...]
            out_refs[slot][...] = (grouped * (gate / (1.0 + jnp.exp(-gate)))).astype(BF16)


def recall(state, steps, lines, decay, bonus, gain, offset):
    heads, span, _, width = state.shape
    depth = span // 2
    column = pl.BlockSpec((span, 1), lambda h, p: (h, 0))
    return pl.pallas_call(
        functools.partial(recall_kernel, steps),
        grid=(heads, span // depth),
        in_specs=[pl.BlockSpec((1, depth, span, width), lambda h, p: (h, p, 0, 0))]
        + [pl.BlockSpec((4, span, width), lambda h, p: (0, h, 0))] * len(lines)
        + [pl.BlockSpec((decay.shape[0], span, width), lambda h, p: (0, h, 0))]
        + [column] * 3,
        out_specs=[pl.BlockSpec((span, width), lambda h, p: (h, 0))] * len(steps),
        out_shape=[jax.ShapeDtypeStruct((heads * span, width), BF16)] * len(steps),
        scratch_shapes=[pltpu.VMEM((len(steps), span, width), F32)] * 2,
        compiler_params=pltpu.CompilerParams(vmem_limit_bytes=60 * 2**20),
        cost_estimate=pl.CostEstimate(
            flops=2 * heads * span * span * width,
            bytes_accessed=4 * heads * span * span * width,
            transcendentals=heads * span * width,
        ),
        name="recall",
    )(state, *lines, decay, bonus, gain, offset)


def renew_kernel(state_ref, *refs):
    line_refs, decay_ref, out_ref, keep_ref, key_ref = refs[:-4], *refs[-4:]
    steps = len(line_refs)
    part = pl.program_id(1)
    depth = state_ref.shape[1]
    width = state_ref.shape[3]

    @pl.when(part == 0)
    def _():
        keep = jnp.ones_like(keep_ref)
        for step in reversed(range(steps)):
            key_ref[step] = line_refs[step][1].astype(F32) * keep
            keep = keep * decay_ref[step]
        keep_ref[...] = keep

    for start in range(0, width, 128):
        lanes = slice(start, start + 128)
        rows = pl.ds(pl.multiple_of(part * depth, depth), depth)
        keep = keep_ref[rows, lanes]
        keys = [key_ref[step, rows, lanes] for step in range(steps)]
        values = [line_refs[step][2, :, lanes].astype(F32) for step in range(steps)]
        for row in range(depth):
            here = slice(row, row + 1)
            total = keep[here] * state_ref[0, row, :, lanes]
            for step in range(steps):
                total = total + keys[step][here] * values[step]
            out_ref[0, row, :, lanes] = total


def renew(state, lines, decay):
    heads, span, _, width = state.shape
    depth = span // 2
    steps = len(lines)
    block = pl.BlockSpec((1, depth, span, width), lambda h, p: (h, p, 0, 0))
    return pl.pallas_call(
        renew_kernel,
        grid=(heads, span // depth),
        in_specs=[block] + [pl.BlockSpec((4, span, width), lambda h, p: (0, h, 0))] * (steps + 1),
        out_specs=block,
        out_shape=jax.ShapeDtypeStruct(state.shape, F32),
        scratch_shapes=[pltpu.VMEM((span, width), F32), pltpu.VMEM((steps, span, width), F32)],
        compiler_params=pltpu.CompilerParams(vmem_limit_bytes=40 * 2**20),
        cost_estimate=pl.CostEstimate(
            flops=9 * heads * span * span * width,
            bytes_accessed=8 * heads * span * span * width,
            transcendentals=0,
        ),
        name="renew",
    )(state, *lines, decay)


def boxed_device(
    sublevel_symbol_entries,
    prior_symbol_memory,
    entry_scaling_multiplier,
    entry_scaling_offset,
    learned_blending,
    blending_lowering_coefficients,
    blending_raising_coefficients,
    fading_lowering_coefficients,
    fading_raising_coefficients,
    learned_fading,
    immediate_item_premium,
    acceptor_projection,
    lookup_projection,
    payload_projection,
    gating_projection,
    emission_projection,
    group_scaling_multiplier,
    group_scaling_offset,
    dialogue_group_memory,
):
    rank = blending_raising_coefficients.shape[1]
    chats, moves, features = sublevel_symbol_entries.shape
    narrow_rows = dialogue_group_memory.shape[1]
    local_width = emission_projection.shape[1]
    groups = local_width // CHANNEL_SPAN
    wide, narrow = lax.axis_index("wide"), lax.axis_index("narrow")
    z, y, x = wide // 4, (wide // 2) % 2, wide % 2
    weights = (acceptor_projection, lookup_projection, payload_projection, gating_projection)

    def in_order(bit, mine, theirs):
        first = bit == 0
        return [jnp.where(first, mine, theirs), jnp.where(first, theirs, mine)]

    def after(value, *earlier):
        return lax.optimization_barrier((value, *earlier))[0]

    order = jnp.stack(
        [
            2 * ((z + PLANES - shift) % PLANES) + row
            for row in (y, 1 - y)
            for shift in range(PLANES)
        ]
        + [narrow]
    ).astype(jnp.int32)

    own_weights = jnp.stack(weights)
    mate_weights = send(own_weights, x_mate)

    def send_z(block, *earlier):
        return [
            send(after(block, *[one[shift - 1] for one in earlier]), z_shift(shift))
            for shift in range(1, PLANES)
        ]

    prior_z = send_z(prior_symbol_memory)

    floats = sublevel_symbol_entries.astype(F32).transpose(1, 0, 2)
    sums = jnp.stack([jnp.sum(floats, -1), jnp.sum(floats * floats, -1)])
    sums = sums + swap(sums)
    center = sums[0][..., None] / FEATURE_EXTENT
    spread = sums[1][..., None] / FEATURE_EXTENT - center * center
    normed = (
        (floats - center) * lax.rsqrt(spread + 1e-05) * entry_scaling_multiplier
        + entry_scaling_offset
    ).astype(BF16)
    previous = jnp.concatenate([prior_symbol_memory[None], normed[:-1]], 0)
    normed_float = normed.astype(F32)
    shifted = previous.astype(F32) - normed_float
    blended = (normed_float + shifted * learned_blending[0]).astype(BF16)
    partial_mix = jnp.einsum(
        "msd,dr->msr", blended, blending_lowering_coefficients, preferred_element_type=F32
    )
    hidden = jnp.tanh(partial_mix + swap(partial_mix)).astype(BF16)
    decay_shift = jnp.einsum(
        "msr,rd->msd",
        hidden[..., :rank],
        blending_raising_coefficients[0],
        preferred_element_type=F32,
    )
    decay_mix = (normed_float + shifted * (learned_blending[1] + decay_shift)).astype(BF16)
    partial_decay = jnp.einsum(
        "msd,dr->msr", decay_mix, fading_lowering_coefficients, preferred_element_type=F32
    )
    decay_hidden = jnp.tanh(partial_decay + swap(partial_decay)).astype(BF16)

    small = jnp.concatenate(
        [hidden[step, :, rank:] for step in range(moves)]
        + [decay_hidden[step] for step in range(moves)],
        1,
    )
    def in_plane(passed):
        passed = jnp.stack((passed[:1] + passed[:0:-1]) * 2)
        return lax.dynamic_slice_in_dim(passed, (PLANES - z) % PLANES, PLANES, 0)

    first = jnp.concatenate([normed[0], normed[1]], 1)
    second = jnp.concatenate([normed[2], normed[3]], 1)
    normed_y = send(jnp.stack([first, second]), y_mate)
    small_z = send_z(small, prior_z)
    prior_y = send(jnp.stack([prior_symbol_memory] + prior_z), y_mate)
    first_z = send_z(first, small_z)
    small_plane = in_plane([small] + small_z)
    small_y = send(small_plane, y_mate)
    first_near_y = send(after(first_z[0], normed_y), y_mate)
    second_z = send_z(second, first_z, (prior_y, small_y, first_near_y))
    first_far_y = send(jnp.stack(first_z[1:]), y_mate)
    second_near_y = send(after(second_z[0], first_near_y), y_mate)
    small_all = jnp.stack(in_order(y, small_plane, small_y), 1).reshape(-1, small.shape[1])

    prior_sources = [(prior_symbol_memory, None, 0)] + [(one, None, 0) for one in prior_z]
    prior_sources += [(prior_y, place, 0) for place in range(PLANES)]

    def first_sources(step):
        found = [(first, None, step)] + [(one, None, step) for one in first_z]
        found += [(normed_y, 0, step), (first_near_y, None, step)]
        return found + [(first_far_y, place, step) for place in range(2)]

    half = small_all.shape[0] // 2
    decay_width = decay_hidden.shape[-1]
    decay_own = lax.dynamic_slice_in_dim(small_all[:, moves * 4 * rank :], narrow * half, half, 0)
    decay_rows = jnp.stack(
        in_order(x, decay_own.reshape(-1, chats, moves * decay_width),
                 send(decay_own, x_mate).reshape(-1, chats, moves * decay_width)),
        1,
    ).reshape(narrow_rows, moves, decay_width)
    decay_log = learned_fading[:, None] + jnp.einsum(
        "rd,smr->mds", fading_raising_coefficients, decay_rows, preferred_element_type=F32
    )
    decay = jnp.exp(-jnp.exp(decay_log))

    blocks = after(emission_projection, normed).reshape(4 * PLANES, local_width, local_width)

    def plane_rows(shift, mates):
        start = ((z + PLANES - shift) % PLANES) * 4
        rows = [
            lax.dynamic_index_in_dim(blocks, start + (wide % 4 ^ mate), 0, False)
            for mate in mates
        ]
        return jnp.concatenate(rows, 0)

    emission_own = plane_rows(0, range(4))
    state = dialogue_group_memory.reshape(groups, CHANNEL_SPAN, CHANNEL_SPAN, narrow_rows)
    bonus = immediate_item_premium[:, None]
    gain = group_scaling_multiplier[:, None]
    offset = group_scaling_offset[:, None]
    mixing_raising = after(blending_raising_coefficients, normed)
    raising = jnp.stack(
        [
            jnp.pad(mixing_raising[kind + 1], ((kind * rank, (3 - kind) * rank), (0, 0)))
            for kind in range(4)
        ]
    )
    blending = learned_blending[2:, None]
    x_here = x.astype(jnp.int32)[None]
    lines = []

    def make(step, nows, befores, *earlier):
        return project(
            after(order, *earlier),
            nows,
            befores,
            small_all[:, step * 4 * rank : (step + 1) * 4 * rank],
            raising,
            blending,
            own_weights,
            mate_weights,
        )

    def pass_on(made, *earlier):
        _, mate_kept, given = made
        theirs = after(mate_kept, *earlier).astype(F32) + given[1].astype(F32)
        theirs = theirs.astype(BF16)
        return theirs, send(theirs, x_mate)

    def line_up(made, arrived, *earlier):
        lines.append(weave(after(x_here, *earlier), made[0], made[2], arrived))
        return lines[-1]

    def read(step, *earlier):
        line = lines[: step + 1]
        gated = recall(state, (step,), line, decay, after(bonus, *earlier), gain, offset)[0]
        gated = jnp.concatenate([gated, send(gated, x_mate)], 0)
        return gated, jnp.concatenate([gated, send(gated, y_mate)], 0)

    def emit(gated, *earlier):
        gated = after(gated, *earlier)
        own = jnp.einsum("cs,ce->se", gated, emission_own, preferred_element_type=F32)
        far = jnp.einsum("cs,ce->se", gated, emission_far, preferred_element_type=F32)
        return own, far.astype(BF16)

    def gather_up(product, *earlier):
        total, far = product
        arrived = [
            send(far[:, shift * local_width : (shift + 1) * local_width], z_shift(shift + 1))
            for shift in range(PLANES - 1)
        ]
        if earlier:
            arrived = after(tuple(arrived), *earlier)
        for one in arrived:
            total = total + one.astype(F32)
        return total.astype(BF16)

    def halves(made):
        return made[0], made[1], swap(made[2])

    made = [halves(make(0, first_sources(0), prior_sources))]
    second_far_y = send(after(jnp.stack(second_z[1:]), made[0][0]), y_mate)

    def second_sources(step):
        found = [(second, None, step)] + [(one, None, step) for one in second_z]
        found += [(normed_y, 1, step), (second_near_y, None, step)]
        return found + [(second_far_y, place, step) for place in range(2)]

    made.append(halves(make(1, first_sources(1), first_sources(0), second_near_y, made[0][0])))
    passed = [pass_on(made[0], made[1][0])]
    emission_z = [
        send(
            after(plane_rows(shift, (2 * narrow, 2 * narrow + 1)), second_z[shift - 1], passed[0][0]),
            z_shift(-shift),
        )
        for shift in range(1, PLANES)
    ]
    passed.append(pass_on(made[1]))
    line_up(made[0], passed[0][1])
    gated = [read(0)]
    made.append(halves(make(2, second_sources(0), first_sources(1), gated[0][0])))
    line_up(made[1], passed[1][1], made[2][0])
    passed.append(pass_on(made[2], lines[1]))
    made.append(
        halves(make(3, second_sources(1), second_sources(0), lines[1], *emission_z))
    )
    emission_near = jnp.concatenate(emission_z, 1)
    emission_far = jnp.concatenate(in_order(narrow, emission_near, swap(emission_near)), 0)
    products = [emit(gated[0][1], made[3][0])]
    results = [gather_up(products[0])]
    passed.append(pass_on(made[3], products[0][1]))
    gated.append(read(1, products[0][1], passed[2][0], passed[3][0]))
    line_up(made[2], passed[2][1], gated[1][0])
    gated.append(read(2))
    line_up(made[3], passed[3][1], gated[2][0])
    products.append(emit(gated[1][1], lines[3]))
    gated.append(read(3, products[1][1], results[0]))
    products.append(emit(gated[2][1], gated[3][0]))
    products.append(emit(gated[3][1], products[2][1]))
    final = renew(after(state, products[3][1]), lines, decay)
    results += [gather_up(products[1]), gather_up(products[2])]
    results.append(gather_up(products[3], final))
    return (
        jnp.stack(results, 1),
        final.reshape(groups * CHANNEL_SPAN * CHANNEL_SPAN, narrow_rows),
    )


def solution(mesh):
    placed = (
        P("wide", None, "narrow"),
        P("wide", "narrow"),
        P("narrow"),
        P("narrow"),
        P(None, "narrow"),
        P("narrow", None),
        P(None, None, "narrow"),
        P("narrow", None),
        P(None, "wide"),
        P("wide"),
        P("wide"),
        P("narrow", "wide"),
        P("narrow", "wide"),
        P("narrow", "wide"),
        P("narrow", "wide"),
        P(None, "wide"),
        P("wide"),
        P("wide"),
        P("wide", "narrow"),
    )
    boxed = mesh.shape["wide"] == PLANES * 4 and mesh.shape["narrow"] == 2
    body = boxed_device if boxed else plain_device
    return jax.shard_map(
        body,
        mesh=mesh,
        in_specs=placed,
        out_specs=(P("narrow", None, "wide"), P("wide", "narrow")),
        check_vma=False,
    )
```

```python
import functools
import jax
import jax.numpy as jnp
from jax import lax
from jax.experimental import pallas as pl
from jax.experimental.pallas import tpu as pltpu
from jax.sharding import PartitionSpec as P

CHANNEL_SPAN = 64
FEATURE_EXTENT = 4096


def plain_device(
    sublevel_symbol_entries,
    prior_symbol_memory,
    entry_scaling_multiplier,
    entry_scaling_offset,
    learned_blending,
    blending_lowering_coefficients,
    blending_raising_coefficients,
    fading_lowering_coefficients,
    fading_raising_coefficients,
    learned_fading,
    immediate_item_premium,
    acceptor_projection,
    lookup_projection,
    payload_projection,
    gating_projection,
    emission_projection,
    group_scaling_multiplier,
    group_scaling_offset,
    dialogue_group_memory,
):
    rank = blending_raising_coefficients.shape[1]
    narrow_rows = dialogue_group_memory.shape[1]
    local_width = emission_projection.shape[1]
    group_partition = local_width // CHANNEL_SPAN
    weights = (acceptor_projection, lookup_projection, payload_projection, gating_projection)
    shift_gathered = lax.all_gather(prior_symbol_memory, "wide", axis=0, tiled=True)

    def channel_set_first(block):
        return block.reshape(narrow_rows, group_partition, CHANNEL_SPAN).transpose(1, 2, 0)

    present_symbol = dialogue_group_memory.reshape(
        group_partition, CHANNEL_SPAN, CHANNEL_SPAN, narrow_rows
    )
    previous_rows = prior_symbol_memory
    previous_all = shift_gathered
    results = []
    for index in range(sublevel_symbol_entries.shape[1]):
        floats = sublevel_symbol_entries[:, index : index + 1].astype(jnp.float32)
        totals, squares = lax.psum((jnp.sum(floats, -1), jnp.sum(floats * floats, -1)), "narrow")
        prepare_center = totals[..., None] / FEATURE_EXTENT
        spread = squares[..., None] / FEATURE_EXTENT - prepare_center * prepare_center
        normed = (
            (floats - prepare_center) * lax.rsqrt(spread + 1e-05) * entry_scaling_multiplier
            + entry_scaling_offset
        ).astype(jnp.bfloat16)
        previous = jnp.concatenate([previous_rows[:, None], normed[:, :-1]], 1)
        prepare_normalized_float = normed.astype(jnp.float32)
        prepare_shifted_input = previous.astype(jnp.float32) - prepare_normalized_float
        blended = (prepare_normalized_float + prepare_shifted_input * learned_blending[0]).astype(
            jnp.bfloat16
        )
        partial_mix = jnp.einsum(
            "smd,dr->smr",
            blended,
            blending_lowering_coefficients,
            preferred_element_type=jnp.float32,
        )
        hidden_activation = jnp.tanh(lax.psum(partial_mix, "narrow")).astype(jnp.bfloat16)
        decay_shift = jnp.einsum(
            "smr,rd->smd",
            hidden_activation[..., :rank],
            blending_raising_coefficients[0],
            preferred_element_type=jnp.float32,
        )
        decay_mix = (
            prepare_normalized_float + prepare_shifted_input * (learned_blending[1] + decay_shift)
        ).astype(jnp.bfloat16)
        partial_decay = jnp.einsum(
            "smd,dr->smr",
            decay_mix,
            fading_lowering_coefficients,
            preferred_element_type=jnp.float32,
        )
        decay_hidden = jnp.tanh(lax.psum(partial_decay, "narrow")).astype(jnp.bfloat16)
        small = jnp.concatenate([hidden_activation[..., rank:], decay_hidden], -1)
        prepare_normed_all = lax.all_gather(normed, "wide", axis=0, tiled=True)
        prepare_small_all = lax.all_gather(small, "wide", axis=0, tiled=True)
        normed, normed_all, small_all = (normed, prepare_normed_all, prepare_small_all)
        project_previous_all = previous_all[:, None]
        normalized_float = normed_all.astype(jnp.float32)
        shifted_input = project_previous_all.astype(jnp.float32) - normalized_float
        term_results = []
        for selector_index in range(4):
            low_rank_update = jnp.einsum(
                "smr,rd->smd",
                small_all[..., selector_index * rank : (selector_index + 1) * rank],
                blending_raising_coefficients[selector_index + 1],
                preferred_element_type=jnp.float32,
            )
            mixed_input = (
                normalized_float
                + shifted_input * (learned_blending[selector_index + 2] + low_rank_update)
            ).astype(jnp.bfloat16)
            term_results.append(
                jnp.einsum(
                    "smd,de->sme",
                    mixed_input,
                    weights[selector_index],
                    preferred_element_type=jnp.float32,
                )
            )
        project_transformed_outcome = lax.psum_scatter(
            jnp.concatenate(term_results, -1).astype(jnp.bfloat16),
            "narrow",
            scatter_dimension=0,
            tiled=True,
        ).astype(jnp.float32)
        rows_start = lax.axis_index("narrow") * narrow_rows
        decay_rows = lax.dynamic_slice_in_dim(
            small_all[..., 4 * rank :], rows_start, narrow_rows, 0
        )
        decay_log = learned_fading + jnp.einsum(
            "smr,rd->smd",
            decay_rows,
            fading_raising_coefficients,
            preferred_element_type=jnp.float32,
        )
        shrink_coefficient = jnp.exp(-jnp.exp(decay_log))
        recurrence_present_symbol = present_symbol
        each_group_reward = immediate_item_premium.reshape(group_partition, CHANNEL_SPAN)
        present_acceptor = channel_set_first(project_transformed_outcome[:, 0, :local_width])
        key_now = channel_set_first(
            project_transformed_outcome[:, 0, local_width : 2 * local_width]
        )
        value_now = channel_set_first(
            project_transformed_outcome[:, 0, 2 * local_width : 3 * local_width]
        )
        gate_now = project_transformed_outcome[:, 0, 3 * local_width :]
        forget_now = channel_set_first(shrink_coefficient[:, 0])
        dyadic_tensor = key_now[:, :, None, :] * value_now[:, None, :, :]
        memory_retrieval = jnp.sum(
            present_acceptor[:, :, None, :]
            * (recurrence_present_symbol + each_group_reward[:, :, None, None] * dyadic_tensor),
            1,
        )
        recurrence_present_symbol = (
            forget_now[:, :, None, :] * recurrence_present_symbol + dyadic_tensor
        )
        center = jnp.mean(memory_retrieval, 1, keepdims=True)
        offset = memory_retrieval - center
        scaled = offset * lax.rsqrt(jnp.mean(offset * offset, 1, keepdims=True) + 0.00064)
        squashed_vector = scaled.transpose(2, 0, 1).reshape(narrow_rows, local_width)
        pieces = [
            (
                (squashed_vector * group_scaling_multiplier + group_scaling_offset)
                * jax.nn.silu(gate_now)
            ).astype(jnp.bfloat16)
        ]
        present_symbol = recurrence_present_symbol
        gated = jnp.stack(pieces, 1)
        results.append(
            jnp.einsum(
                "smc,ce->sme",
                lax.all_gather(gated, "wide", axis=2, tiled=True),
                emission_projection,
                preferred_element_type=jnp.float32,
            ).astype(jnp.bfloat16)
        )
        previous_rows = normed[:, 0]
        previous_all = normed_all[:, 0]
    mixing_output = jnp.concatenate(results, 1)
    return (
        mixing_output,
        present_symbol.reshape(group_partition * CHANNEL_SPAN * CHANNEL_SPAN, narrow_rows),
    )


PLANES = 4
F32 = jnp.float32
BF16 = jnp.bfloat16


def pairs(move):
    moved = [(here, move(here)) for here in range(4 * PLANES)]
    return [(here, there) for here, there in moved if there is not None]


def x_mate(here):
    return here ^ 1


def y_mate(here):
    return here ^ 2


def z_shift(amount):
    return lambda here: (here + 4 * amount) % (4 * PLANES)


def send(block, move):
    return lax.ppermute(block, "wide", pairs(move))


def swap(block):
    return lax.ppermute(block, "narrow", [(0, 1), (1, 0)])


def project_kernel(order_ref, *refs):
    nows, befores, refs = refs[:8], refs[8:16], refs[16:]
    small_ref, raise_ref, blend_ref, own_ref, mate_ref, *refs = refs
    kept_refs, given_ref, now_ref, shift_ref, mix_ref = refs[:2], *refs[2:]
    rows = nows[0].shape[0]
    half, features = given_ref.shape[2], now_ref.shape[1]
    first = order_ref[8] == 0

    @pl.when(pl.program_id(0) == 0)
    def _():
        for block in range(8):
            here = pl.ds(pl.multiple_of(order_ref[block] * rows, rows), rows)
            now = nows[block][...]
            now_ref[here, :] = now
            shift_ref[here, :] = befores[block][...].astype(F32) - now.astype(F32)

    for start in range(0, features, 512):
        here = slice(start, start + 512)
        low = jnp.dot(small_ref[...], raise_ref[0, :, here], preferred_element_type=F32)
        mixed = now_ref[:, here].astype(F32) + shift_ref[:, here] * (blend_ref[0, :, here] + low)
        mix_ref[:, here] = mixed.astype(BF16)
    for side, weight_ref in enumerate((own_ref, mate_ref)):
        total = jnp.dot(mix_ref[...], weight_ref[0], preferred_element_type=F32).astype(BF16)
        kept_refs[side][0] = jnp.where(first, total[:half], total[half:])
        given_ref[side, 0] = jnp.where(first, total[half:], total[:half])


def project(order, nows, befores, small, raising, blending, own, mate):
    columns, features = own.shape[2], own.shape[1]
    rows = nows[0][0].shape[-2]
    total = 8 * rows

    def spec(source):
        array, place, column = source
        if place is None:
            return pl.BlockSpec((rows, features), lambda c, order: (0, column))
        return pl.BlockSpec((None, rows, features), lambda c, order: (place, 0, column))

    kind = lambda shape: pl.BlockSpec((1,) + shape[1:], lambda c, order: (c, 0, 0))
    sources = list(nows) + list(befores)
    return pl.pallas_call(
        project_kernel,
        grid_spec=pltpu.PrefetchScalarGridSpec(
            num_scalar_prefetch=1,
            grid=(4,),
            in_specs=[spec(source) for source in sources]
            + [pl.BlockSpec(small.shape, lambda c, order: (0, 0))]
            + [kind(raising.shape), kind(blending.shape), kind(own.shape), kind(mate.shape)],
            out_specs=[pl.BlockSpec((1, total // 2, columns), lambda c, order: (c, 0, 0))] * 2
            + [pl.BlockSpec((2, 1, total // 2, columns), lambda c, order: (0, c, 0, 0))],
            scratch_shapes=[
                pltpu.VMEM((total, features), BF16),
                pltpu.VMEM((total, features), F32),
                pltpu.VMEM((total, features), BF16),
            ],
        ),
        out_shape=[jax.ShapeDtypeStruct((4, total // 2, columns), BF16)] * 2
        + [jax.ShapeDtypeStruct((2, 4, total // 2, columns), BF16)],
        compiler_params=pltpu.CompilerParams(vmem_limit_bytes=60 * 2**20),
        cost_estimate=pl.CostEstimate(
            flops=2 * total * features * columns * 12,
            bytes_accessed=16 * features * columns + 4 * total * features,
            transcendentals=0,
        ),
        name="project",
    )(order, *[source[0] for source in sources], small, raising, blending, own, mate)


def weave_kernel(x_ref, kept_ref, given_ref, mate_ref, out_ref):
    chats = mate_ref.shape[1] // 4
    own = (kept_ref[0].astype(F32) + given_ref[0, 0].astype(F32)).astype(BF16)
    mate = mate_ref[0]
    first = x_ref[0] == 0
    for block in range(4):
        rows = slice(block * chats, (block + 1) * chats)
        low = jnp.where(first, own[rows], mate[rows])
        high = jnp.where(first, mate[rows], own[rows])
        lanes = slice(2 * block * chats, 2 * (block + 1) * chats)
        out_ref[0, :, lanes] = jnp.concatenate([low, high], 0).T


def weave(x, kept, given, mate):
    _, half, columns = kept.shape
    side = pl.BlockSpec((1, half, columns), lambda c, x: (c, 0, 0))
    return pl.pallas_call(
        weave_kernel,
        grid_spec=pltpu.PrefetchScalarGridSpec(
            num_scalar_prefetch=1,
            grid=(4,),
            in_specs=[side, pl.BlockSpec((1, 1, half, columns), lambda c, x: (0, c, 0, 0)), side],
            out_specs=pl.BlockSpec((1, columns, 2 * half), lambda c, x: (c, 0, 0)),
        ),
        out_shape=jax.ShapeDtypeStruct((4, columns, 2 * half), BF16),
        cost_estimate=pl.CostEstimate(
            flops=8 * half * columns, bytes_accessed=64 * half * columns, transcendentals=0
        ),
        name="weave",
    )(x, kept, given, mate)


def recall_kernel(steps, *refs):
    last = steps[-1]
    state_ref, line_refs, refs = refs[0], refs[1 : 2 + last], refs[2 + last :]
    decay_ref, bonus_ref, gain_ref, offset_ref = refs[:4]
    out_refs, (reach_ref, total_ref) = refs[4:-2], refs[-2:]
    part = pl.program_id(1)
    depth = state_ref.shape[1]
    span = state_ref.shape[2]
    width = state_ref.shape[3]

    @pl.when(part == 0)
    def _():
        for slot, step in enumerate(steps):
            reach = line_refs[step][0].astype(F32)
            for earlier in range(step):
                reach = reach * decay_ref[earlier]
            reach_ref[slot] = reach
        total_ref[...] = jnp.zeros_like(total_ref)

    for start in range(0, width, 128):
        lanes = slice(start, start + 128)
        here = pl.ds(pl.multiple_of(part * depth, depth), depth)
        totals = [total_ref[slot, :, lanes] for slot in range(len(steps))]
        reaches = [reach_ref[slot, here, lanes] for slot in range(len(steps))]
        for row in range(depth):
            memory = state_ref[0, row, :, lanes]
            for slot in range(len(steps)):
                totals[slot] = totals[slot] + reaches[slot][row : row + 1, :] * memory
        for slot in range(len(steps)):
            total_ref[slot, :, lanes] = totals[slot]

    @pl.when(part == pl.num_programs(1) - 1)
    def _():
        for slot, step in enumerate(steps):
            now_ref = line_refs[step]
            acceptor = now_ref[0].astype(F32)
            readout = total_ref[slot]
            weight = jnp.sum(acceptor * bonus_ref[...] * now_ref[1].astype(F32), 0, keepdims=True)
            readout = readout + weight * now_ref[2].astype(F32)
            for earlier in reversed(range(step)):
                weight = jnp.sum(acceptor * line_refs[earlier][1].astype(F32), 0, keepdims=True)
                readout = readout + weight * line_refs[earlier][2].astype(F32)
                if earlier:
                    acceptor = acceptor * decay_ref[earlier]
            center = jnp.sum(readout, 0, keepdims=True) * (1.0 / span)
            offset = readout - center
            spread = jnp.sum(offset * offset, 0, keepdims=True) * (1.0 / span)
            scaled = offset * lax.rsqrt(spread + 0.00064)
            gate = now_ref[3].astype(F32)
            grouped = scaled * gain_ref[...] + offset_ref[...]
            out_refs[slot][...] = (grouped * (gate / (1.0 + jnp.exp(-gate)))).astype(BF16)


def recall(state, steps, lines, decay, bonus, gain, offset):
    heads, span, _, width = state.shape
    depth = span // 2
    column = pl.BlockSpec((span, 1), lambda h, p: (h, 0))
    return pl.pallas_call(
        functools.partial(recall_kernel, steps),
        grid=(heads, span // depth),
        in_specs=[pl.BlockSpec((1, depth, span, width), lambda h, p: (h, p, 0, 0))]
        + [pl.BlockSpec((4, span, width), lambda h, p: (0, h, 0))] * len(lines)
        + [pl.BlockSpec((decay.shape[0], span, width), lambda h, p: (0, h, 0))]
        + [column] * 3,
        out_specs=[pl.BlockSpec((span, width), lambda h, p: (h, 0))] * len(steps),
        out_shape=[jax.ShapeDtypeStruct((heads * span, width), BF16)] * len(steps),
        scratch_shapes=[pltpu.VMEM((len(steps), span, width), F32)] * 2,
        compiler_params=pltpu.CompilerParams(vmem_limit_bytes=60 * 2**20),
        cost_estimate=pl.CostEstimate(
            flops=2 * heads * span * span * width,
            bytes_accessed=4 * heads * span * span * width,
            transcendentals=heads * span * width,
        ),
        name="recall",
    )(state, *lines, decay, bonus, gain, offset)


def renew_kernel(state_ref, *refs):
    line_refs, decay_ref, out_ref, keep_ref, key_ref = refs[:-4], *refs[-4:]
    steps = len(line_refs)
    part = pl.program_id(1)
    depth = state_ref.shape[1]
    width = state_ref.shape[3]

    @pl.when(part == 0)
    def _():
        keep = jnp.ones_like(keep_ref)
        for step in reversed(range(steps)):
            key_ref[step] = line_refs[step][1].astype(F32) * keep
            keep = keep * decay_ref[step]
        keep_ref[...] = keep

    for start in range(0, width, 128):
        lanes = slice(start, start + 128)
        rows = pl.ds(pl.multiple_of(part * depth, depth), depth)
        keep = keep_ref[rows, lanes]
        keys = [key_ref[step, rows, lanes] for step in range(steps)]
        values = [line_refs[step][2, :, lanes].astype(F32) for step in range(steps)]
        for row in range(depth):
            here = slice(row, row + 1)
            total = keep[here] * state_ref[0, row, :, lanes]
            for step in range(steps):
                total = total + keys[step][here] * values[step]
            out_ref[0, row, :, lanes] = total


def renew(state, lines, decay):
    heads, span, _, width = state.shape
    depth = span // 2
    steps = len(lines)
    block = pl.BlockSpec((1, depth, span, width), lambda h, p: (h, p, 0, 0))
    return pl.pallas_call(
        renew_kernel,
        grid=(heads, span // depth),
        in_specs=[block] + [pl.BlockSpec((4, span, width), lambda h, p: (0, h, 0))] * (steps + 1),
        out_specs=block,
        out_shape=jax.ShapeDtypeStruct(state.shape, F32),
        scratch_shapes=[pltpu.VMEM((span, width), F32), pltpu.VMEM((steps, span, width), F32)],
        compiler_params=pltpu.CompilerParams(vmem_limit_bytes=40 * 2**20),
        cost_estimate=pl.CostEstimate(
            flops=9 * heads * span * span * width,
            bytes_accessed=8 * heads * span * span * width,
            transcendentals=0,
        ),
        name="renew",
    )(state, *lines, decay)


def boxed_device(
    sublevel_symbol_entries,
    prior_symbol_memory,
    entry_scaling_multiplier,
    entry_scaling_offset,
    learned_blending,
    blending_lowering_coefficients,
    blending_raising_coefficients,
    fading_lowering_coefficients,
    fading_raising_coefficients,
    learned_fading,
    immediate_item_premium,
    acceptor_projection,
    lookup_projection,
    payload_projection,
    gating_projection,
    emission_projection,
    group_scaling_multiplier,
    group_scaling_offset,
    dialogue_group_memory,
):
    rank = blending_raising_coefficients.shape[1]
    chats, moves, features = sublevel_symbol_entries.shape
    narrow_rows = dialogue_group_memory.shape[1]
    local_width = emission_projection.shape[1]
    groups = local_width // CHANNEL_SPAN
    wide, narrow = lax.axis_index("wide"), lax.axis_index("narrow")
    z, y, x = wide // 4, (wide // 2) % 2, wide % 2
    weights = (acceptor_projection, lookup_projection, payload_projection, gating_projection)

    def in_order(bit, mine, theirs):
        first = bit == 0
        return [jnp.where(first, mine, theirs), jnp.where(first, theirs, mine)]

    def after(value, *earlier):
        return lax.optimization_barrier((value, *earlier))[0]

    order = jnp.stack(
        [
            2 * ((z + PLANES - shift) % PLANES) + row
            for row in (y, 1 - y)
            for shift in range(PLANES)
        ]
        + [narrow]
    ).astype(jnp.int32)

    own_weights = jnp.stack(weights)
    mate_weights = send(own_weights, x_mate)

    def send_z(block, *earlier):
        return [
            send(after(block, *[one[shift - 1] for one in earlier]), z_shift(shift))
            for shift in range(1, PLANES)
        ]

    prior_z = send_z(prior_symbol_memory)

    floats = sublevel_symbol_entries.astype(F32).transpose(1, 0, 2)
    sums = jnp.stack([jnp.sum(floats, -1), jnp.sum(floats * floats, -1)])
    sums = sums + swap(sums)
    center = sums[0][..., None] / FEATURE_EXTENT
    spread = sums[1][..., None] / FEATURE_EXTENT - center * center
    normed = (
        (floats - center) * lax.rsqrt(spread + 1e-05) * entry_scaling_multiplier
        + entry_scaling_offset
    ).astype(BF16)
    previous = jnp.concatenate([prior_symbol_memory[None], normed[:-1]], 0)
    normed_float = normed.astype(F32)
    shifted = previous.astype(F32) - normed_float
    blended = (normed_float + shifted * learned_blending[0]).astype(BF16)
    partial_mix = jnp.einsum(
        "msd,dr->msr", blended, blending_lowering_coefficients, preferred_element_type=F32
    )
    hidden = jnp.tanh(partial_mix + swap(partial_mix)).astype(BF16)
    decay_shift = jnp.einsum(
        "msr,rd->msd",
        hidden[..., :rank],
        blending_raising_coefficients[0],
        preferred_element_type=F32,
    )
    decay_mix = (normed_float + shifted * (learned_blending[1] + decay_shift)).astype(BF16)
    partial_decay = jnp.einsum(
        "msd,dr->msr", decay_mix, fading_lowering_coefficients, preferred_element_type=F32
    )
    decay_hidden = jnp.tanh(partial_decay + swap(partial_decay)).astype(BF16)

    small = jnp.concatenate(
        [hidden[step, :, rank:] for step in range(moves)]
        + [decay_hidden[step] for step in range(moves)],
        1,
    )
    def in_plane(passed):
        passed = jnp.stack((passed[:1] + passed[:0:-1]) * 2)
        return lax.dynamic_slice_in_dim(passed, (PLANES - z) % PLANES, PLANES, 0)

    first = jnp.concatenate([normed[0], normed[1]], 1)
    second = jnp.concatenate([normed[2], normed[3]], 1)
    normed_y = send(jnp.stack([first, second]), y_mate)
    small_z = send_z(small, prior_z)
    prior_y = send(jnp.stack([prior_symbol_memory] + prior_z), y_mate)
    first_z = send_z(first, small_z)
    small_plane = in_plane([small] + small_z)
    small_y = send(small_plane, y_mate)
    first_near_y = send(after(first_z[0], normed_y), y_mate)
    second_z = send_z(second, first_z, (prior_y, small_y, first_near_y))
    first_far_y = send(jnp.stack(first_z[1:]), y_mate)
    second_near_y = send(after(second_z[0], first_near_y), y_mate)
    small_all = jnp.stack(in_order(y, small_plane, small_y), 1).reshape(-1, small.shape[1])

    prior_sources = [(prior_symbol_memory, None, 0)] + [(one, None, 0) for one in prior_z]
    prior_sources += [(prior_y, place, 0) for place in range(PLANES)]

    def first_sources(step):
        found = [(first, None, step)] + [(one, None, step) for one in first_z]
        found += [(normed_y, 0, step), (first_near_y, None, step)]
        return found + [(first_far_y, place, step) for place in range(2)]

    half = small_all.shape[0] // 2
    decay_width = decay_hidden.shape[-1]
    decay_own = lax.dynamic_slice_in_dim(small_all[:, moves * 4 * rank :], narrow * half, half, 0)
    decay_rows = jnp.stack(
        in_order(x, decay_own.reshape(-1, chats, moves * decay_width),
                 send(decay_own, x_mate).reshape(-1, chats, moves * decay_width)),
        1,
    ).reshape(narrow_rows, moves, decay_width)
    decay_log = learned_fading[:, None] + jnp.einsum(
        "rd,smr->mds", fading_raising_coefficients, decay_rows, preferred_element_type=F32
    )
    decay = jnp.exp(-jnp.exp(decay_log))

    blocks = after(emission_projection, normed).reshape(4 * PLANES, local_width, local_width)

    def plane_rows(shift, mates):
        start = ((z + PLANES - shift) % PLANES) * 4
        rows = [
            lax.dynamic_index_in_dim(blocks, start + (wide % 4 ^ mate), 0, False)
            for mate in mates
        ]
        return jnp.concatenate(rows, 0)

    emission_own = plane_rows(0, range(4))
    state = dialogue_group_memory.reshape(groups, CHANNEL_SPAN, CHANNEL_SPAN, narrow_rows)
    bonus = immediate_item_premium[:, None]
    gain = group_scaling_multiplier[:, None]
    offset = group_scaling_offset[:, None]
    mixing_raising = after(blending_raising_coefficients, normed)
    raising = jnp.stack(
        [
            jnp.pad(mixing_raising[kind + 1], ((kind * rank, (3 - kind) * rank), (0, 0)))
            for kind in range(4)
        ]
    )
    blending = learned_blending[2:, None]
    x_here = x.astype(jnp.int32)[None]
    lines = []

    def make(step, nows, befores, *earlier):
        return project(
            after(order, *earlier),
            nows,
            befores,
            small_all[:, step * 4 * rank : (step + 1) * 4 * rank],
            raising,
            blending,
            own_weights,
            mate_weights,
        )

    def pass_on(made, *earlier):
        _, mate_kept, given = made
        theirs = after(mate_kept, *earlier).astype(F32) + given[1].astype(F32)
        theirs = theirs.astype(BF16)
        return theirs, send(theirs, x_mate)

    def line_up(made, arrived, *earlier):
        lines.append(weave(after(x_here, *earlier), made[0], made[2], arrived))
        return lines[-1]

    def read(step, *earlier):
        line = lines[: step + 1]
        gated = recall(state, (step,), line, decay, after(bonus, *earlier), gain, offset)[0]
        gated = jnp.concatenate([gated, send(gated, x_mate)], 0)
        return gated, jnp.concatenate([gated, send(gated, y_mate)], 0)

    def emit(gated, *earlier):
        gated = after(gated, *earlier)
        own = jnp.einsum("cs,ce->se", gated, emission_own, preferred_element_type=F32)
        far = jnp.einsum("cs,ce->se", gated, emission_far, preferred_element_type=F32)
        return own, far.astype(BF16)

    def gather_up(product, *earlier):
        total, far = product
        arrived = [
            send(far[:, shift * local_width : (shift + 1) * local_width], z_shift(shift + 1))
            for shift in range(PLANES - 1)
        ]
        if earlier:
            arrived = after(tuple(arrived), *earlier)
        for one in arrived:
            total = total + one.astype(F32)
        return total.astype(BF16)

    def halves(made):
        return made[0], made[1], swap(made[2])

    made = [halves(make(0, first_sources(0), prior_sources))]
    second_far_y = send(after(jnp.stack(second_z[1:]), made[0][0]), y_mate)

    def second_sources(step):
        found = [(second, None, step)] + [(one, None, step) for one in second_z]
        found += [(normed_y, 1, step), (second_near_y, None, step)]
        return found + [(second_far_y, place, step) for place in range(2)]

    made.append(halves(make(1, first_sources(1), first_sources(0), second_near_y, made[0][0])))
    passed = [pass_on(made[0], made[1][0])]
    emission_z = [
        send(
            after(plane_rows(shift, (2 * narrow, 2 * narrow + 1)), second_z[shift - 1], passed[0][0]),
            z_shift(-shift),
        )
        for shift in range(1, PLANES)
    ]
    passed.append(pass_on(made[1]))
    line_up(made[0], passed[0][1])
    gated = [read(0)]
    made.append(halves(make(2, second_sources(0), first_sources(1), gated[0][0])))
    line_up(made[1], passed[1][1], made[2][0])
    passed.append(pass_on(made[2], lines[1]))
    made.append(
        halves(make(3, second_sources(1), second_sources(0), lines[1], *emission_z))
    )
    emission_near = jnp.concatenate(emission_z, 1)
    emission_far = jnp.concatenate(in_order(narrow, emission_near, swap(emission_near)), 0)
    products = [emit(gated[0][1], made[3][0])]
    results = [gather_up(products[0])]
    passed.append(pass_on(made[3], products[0][1]))
    gated.append(read(1, products[0][1], passed[2][0], passed[3][0]))
    line_up(made[2], passed[2][1], gated[1][0])
    gated.append(read(2))
    line_up(made[3], passed[3][1], gated[2][0])
    products.append(emit(gated[1][1], lines[3]))
    gated.append(read(3, products[1][1], results[0]))
    products.append(emit(gated[2][1], gated[3][0]))
    products.append(emit(gated[3][1], products[2][1]))
    final = renew(after(state, products[3][1]), lines, decay)
    results += [gather_up(products[1]), gather_up(products[2])]
    results.append(gather_up(products[3], final))
    return (
        jnp.stack(results, 1),
        final.reshape(groups * CHANNEL_SPAN * CHANNEL_SPAN, narrow_rows),
    )


def solution(mesh):
    placed = (
        P("wide", None, "narrow"),
        P("wide", "narrow"),
        P("narrow"),
        P("narrow"),
        P(None, "narrow"),
        P("narrow", None),
        P(None, None, "narrow"),
        P("narrow", None),
        P(None, "wide"),
        P("wide"),
        P("wide"),
        P("narrow", "wide"),
        P("narrow", "wide"),
        P("narrow", "wide"),
        P("narrow", "wide"),
        P(None, "wide"),
        P("wide"),
        P("wide"),
        P("wide", "narrow"),
    )
    boxed = mesh.shape["wide"] == PLANES * 4 and mesh.shape["narrow"] == 2
    body = boxed_device if boxed else plain_device
    return jax.shard_map(
        body,
        mesh=mesh,
        in_specs=placed,
        out_specs=(P("narrow", None, "wide"), P("wide", "narrow")),
        check_vma=False,
    )
```
